256 devices in a mesh: ctx: 64 (over x, y, z_lo), tp: 4 (over z_hi, core).
Axes of the slice: x: 4, y: 4, z: 8 (z_hi: 2, z_lo: 4; z = z_hi * 4 + z_lo), core: 2. Of those that a mesh axis runs over, the one named last changes fastest.
Arguments:
- hidden: bfloat16 [32768, 8192], P('ctx'), may hold values from -32 to 32, as said below
- w_query: bfloat16 [8192, 4096], P('ctx', 'tp'), may hold values from -0.0625 to 0.0625
- w_key: bfloat16 [8192, 512], P('ctx', 'tp'), may hold values from -0.0625 to 0.0625
- w_value: bfloat16 [8192, 512], P('ctx', 'tp'), may hold values from -0.0625 to 0.0625
- block_order: int32 [64], replicated, may hold values from 0 to 63, each once
- page_map: int32 [4096, 1], replicated, may hold values from 0 to 63; in each aligned block of 64 rows (0 to 63, 64 to 127, ...) at most 2 rows name the same one
Outputs:
- attended: bfloat16 [32768, 4096], P('ctx', 'tp')
- kv_cache: bfloat16 [64, 64, 2, 8, 1024], P('ctx', None, None, None, 'tp')
The draws below stay inside these ranges and needn't reach their ends.
Inputs may be any that keep to these rules, and one draw needn't show every extreme that they name: `hidden`: drawn activations; no further structure. `page_map`: among the 64 pages of one block, at most 2 share an owner, and in every draw some block has 2 pages with one owner. `block_order`: each block number appears once.
All inputs are finite; a program needn't handle non-finite values.
Results may differ from the reference program's by a relative error of at most 0.012.
The reference program's roundings to bfloat16 on the way (of `weights`) count: a program that leaves them out, or rounds other values in their place, can miss the bound.
Values may be sent and summed in bfloat16 or wider, within the bound.
A program may use at most 128 MiB of HBM per device.

```python
import math
import jax
import jax.numpy as jnp
import numpy as np
from jax import lax

D = 8192
HEADS = 32
KV_HEADS = 4
HD = 128
TOK_DEV = 512
PAGE = 8
PPB = 64
CAP = 2
TOKENS = 32768
N_CTX = 64


def draw_hidden(key, part):
    key = jax.random.fold_in(key, 11)
    base_key = jax.random.fold_in(key, 0)
    values = jnp.clip(jax.random.normal(base_key, (TOKENS, D), jnp.float32), -5.0, 5.0)
    return values.astype(jnp.bfloat16)


def levels(rng, shape, cuts, low, largest):
    def one(dim, shards_of):
        draws = jax.random.uniform(jax.random.fold_in(jax.random.fold_in(rng, 6), dim), (shards_of,), jnp.float32, low / len(cuts), largest / len(cuts))
        return jnp.repeat(jnp.exp(draws), shape[dim] // shards_of).reshape((-1,) + (1,) * (len(shape) - dim - 1))

    loudness = one(*cuts[0])
    for cut in cuts[1:]:
        loudness = loudness * one(*cut)
    return loudness


def deal_out(key, own, number, rows, count, top, most, skew):
    ranking = jax.random.permutation(key, count)
    heavy_load, common = portions_of(count, rows * top, most, skew, True), portions_of(count, rows * top, most, skew, False)
    places = jnp.arange(count)

    def named(lengths, rotation):
        used = int((lengths > 0).sum())
        fixed = max(1, used // 4)
        passed = fixed + (places - fixed + rotation * (used - fixed)) % max(1, count - fixed)
        return jnp.zeros((count,), jnp.int32).at[ranking[jnp.where(places < fixed, places, passed)]].set(jnp.asarray(lengths, jnp.int32))

    lengths = jnp.where(number % 4 == 0, named(heavy_load, number // 4), named(common, number - number // 4 - 1))
    mixed = jax.random.permutation(jax.random.fold_in(own, 3), count)
    donor, taker = mixed[0:count // 2 * 2:2], mixed[1:count // 2 * 2:2]
    slack = jnp.minimum(lengths[donor] - 1, most - lengths[taker]) // 2
    slack = jnp.where((donor == ranking[0]) | (taker == ranking[0]) | (lengths[taker] == 0), 0, jnp.maximum(slack, 0))
    passed = jax.random.randint(jax.random.fold_in(own, 4), (count // 2,), 0, 1 << 20) % (slack + 1)
    lengths = lengths.at[donor].add(-passed).at[taker].add(passed)
    items = jnp.searchsorted(jnp.cumsum(lengths), jnp.arange(rows * top), side="right").astype(jnp.int32)
    listing = items.reshape(top, rows).T
    listing = listing[jax.random.permutation(jax.random.fold_in(own, 1), rows)]
    rotation = jax.random.randint(jax.random.fold_in(own, 2), (rows, 1), 0, top)
    return jnp.take_along_axis(listing, (jnp.arange(top)[None, :] + rotation) % top, axis=1)


def portions_of(count, total, most, lean, full):
    weights = [(1 << 20) // math.isqrt(grade ** lean) + 1 for grade in range(1, count + 1)]
    largest = most if full else min(most, max(-(-total // count), total * weights[0] // sum(weights)))
    least = 1 if total - largest >= count - 1 else 0
    given, spare = [largest] + [least] * (count - 1), total - largest - least * (count - 1)
    while spare > 0:
        free = [i for i in range(1, count) if given[i] < largest] or [i for i in range(1, count) if given[i] < most]
        pool, remaining = sum([weights[i] for i in free]), spare
        for i in free:
            more = min(most - given[i], max(1, remaining * weights[i] // pool), spare)
            given[i] = given[i] + more
            spare = spare - more
    return np.array(given)


def centred(rng, extent, deviation, reach, pieces=(), kind=jnp.bfloat16):
    loudness = levels(rng, extent, pieces, -0.22, 0.18) if pieces else 1.0
    array = jax.random.normal(rng, extent, jnp.float32) * deviation * loudness
    return jnp.minimum(jnp.maximum(array, -reach), reach).astype(kind)


def setup_inputs(seed: int = 0) -> dict:
    key_list = jax.random.split(jax.random.key(seed), 7)
    hidden = draw_hidden(jax.random.fold_in(key_list[6], 71), 0)
    w_query = centred(key_list[1], (D, HEADS * HD), D ** -0.5, 0.0625, ((0, 64), (1, 4)))
    w_key = centred(key_list[2], (D, KV_HEADS * HD), D ** -0.5, 0.0625, ((0, 64), (1, 4)))
    w_value = centred(key_list[3], (D, KV_HEADS * HD), D ** -0.5, 0.0625, ((0, 64), (1, 4)))
    block_order = jax.random.permutation(key_list[4], N_CTX).astype(jnp.int32)
    page_map_keys = jax.random.split(jax.random.fold_in(key_list[5], 1), (N_CTX * PPB) // PPB)
    page_map_turns = jax.random.permutation(jax.random.fold_in(key_list[5], 3), (N_CTX * PPB) // PPB)
    page_map = jax.vmap(lambda own, number: deal_out(jax.random.fold_in(key_list[5], 2), own, number, PPB, N_CTX, 1, CAP, 2))(page_map_keys, page_map_turns).reshape((N_CTX * PPB, 1))
    return {"hidden": hidden, "w_query": w_query, "w_key": w_key, "w_value": w_value, "block_order": block_order, "page_map": page_map}


rope_theta = 500000.0
neg_large = -1e+30

def rotate(values, positions):
    half_width = values.shape[-1] // 2
    exponent = jnp.arange(half_width, dtype=jnp.float32) * (2.0 / values.shape[-1])
    inverse = jnp.exp(-exponent * jnp.log(jnp.float32(rope_theta)))
    angles = positions[:, None] * inverse[None, :]
    cosine = jnp.cos(angles)
    sine = jnp.sin(angles)
    cosine = jnp.concatenate([cosine, cosine], -1)[:, None, :]
    sine = jnp.concatenate([sine, sine], -1)[:, None, :]
    lower_half = values[..., :half_width]
    upper_half = values[..., half_width:]
    turned = jnp.concatenate([-upper_half, lower_half], -1)
    return values * cosine + turned * sine

def attend_block(query_block, key_block, value_block, anchor_key, anchor_value, is_anchor):
    row_count = query_block.shape[0]
    score_scale = 1.0 / jnp.sqrt(jnp.float32(query_block.shape[-1]))
    own = jnp.einsum('rkgd,skd->kgrs', query_block.astype(jnp.float32), key_block.astype(jnp.float32)) * score_scale
    causal = jnp.arange(row_count)[:, None] >= jnp.arange(row_count)[None, :]
    own = jnp.where(causal, own, neg_large)
    far = jnp.einsum('rkgd,skd->kgrs', query_block.astype(jnp.float32), anchor_key.astype(jnp.float32)) * score_scale
    far = jnp.where(is_anchor, neg_large, far)
    top = jnp.maximum(lax.optimization_barrier(jnp.max(own, -1)), lax.optimization_barrier(jnp.max(far, -1)))
    own_exp = jnp.exp(own - top[..., None])
    far_exp = jnp.exp(far - top[..., None])
    total = lax.optimization_barrier(jnp.sum(own_exp, -1)) + lax.optimization_barrier(jnp.sum(far_exp, -1))
    own_weights = (own_exp / total[..., None]).astype(jnp.bfloat16)
    far_weights = (far_exp / total[..., None]).astype(jnp.bfloat16)
    result = jnp.einsum('kgrs,skd->rkgd', own_weights.astype(jnp.float32), value_block.astype(jnp.float32))
    result = result + jnp.einsum('kgrs,skd->rkgd', far_weights.astype(jnp.float32), anchor_value.astype(jnp.float32))
    return result.reshape(row_count, -1).astype(jnp.bfloat16)

def reference(hidden, w_query, w_key, w_value, block_order, page_map):
    group_size = HEADS // KV_HEADS
    queries = jnp.dot(hidden, w_query, preferred_element_type=jnp.float32).reshape(TOKENS, HEADS, HD)
    keys_raw = jnp.dot(hidden, w_key, preferred_element_type=jnp.float32).reshape(TOKENS, KV_HEADS, HD)
    value_heads = jnp.dot(hidden, w_value, preferred_element_type=jnp.float32).reshape(TOKENS, KV_HEADS, HD).astype(jnp.bfloat16)
    row_blocks = jnp.repeat(block_order, TOK_DEV)
    positions = (row_blocks * TOK_DEV + jnp.tile(jnp.arange(TOK_DEV, dtype=jnp.int32), N_CTX)).astype(jnp.float32)
    query_heads = rotate(queries, positions).astype(jnp.bfloat16)
    key_heads = rotate(keys_raw, positions).astype(jnp.bfloat16)
    root_index = jnp.sum(jnp.where(block_order == 0, jnp.arange(N_CTX, dtype=jnp.int32), 0)).astype(jnp.int32)
    anchor_key = lax.dynamic_slice_in_dim(key_heads, root_index * TOK_DEV, TOK_DEV, 0)
    anchor_value = lax.dynamic_slice_in_dim(value_heads, root_index * TOK_DEV, TOK_DEV, 0)

    def one_block(index):
        start = (index * TOK_DEV).astype(jnp.int32)
        query_block = lax.dynamic_slice_in_dim(query_heads, start, TOK_DEV, 0).reshape(TOK_DEV, KV_HEADS, group_size, HD)
        key_block = lax.dynamic_slice_in_dim(key_heads, start, TOK_DEV, 0)
        value_block = lax.dynamic_slice_in_dim(value_heads, start, TOK_DEV, 0)
        return attend_block(query_block, key_block, value_block, anchor_key, anchor_value, block_order[index] == 0)
    attended = lax.map(one_block, jnp.arange(N_CTX, dtype=jnp.int32)).reshape(TOKENS, HEADS * HD)
    width = KV_HEADS * 2 * HD
    pair_pack = jnp.concatenate([key_heads, value_heads], -1).reshape(N_CTX, PPB, PAGE, width)
    owners = page_map[:, 0].reshape(N_CTX, PPB)[block_order]
    before = jnp.arange(PPB)[None, :] < jnp.arange(PPB)[:, None]
    earlier = (owners[:, :, None] == owners[:, None, :]) & before[None, :, :]
    slot_rank = lax.optimization_barrier(jnp.sum(jnp.where(earlier, 1, 0), axis=-1)).astype(jnp.int32)
    block_index = jnp.broadcast_to(block_order[:, None], (N_CTX, PPB)).astype(jnp.int32)
    kv_cache = jnp.zeros((N_CTX, N_CTX, CAP, PAGE, width), jnp.bfloat16)
    kv_cache = kv_cache.at[owners, block_index, slot_rank].set(pair_pack)
    return (attended, kv_cache)
```

```python
import functools
import math

import jax
import jax.numpy as jnp
from jax import lax
from jax.experimental import pallas as pl
from jax.experimental.pallas import tpu as pltpu
from jax.sharding import PartitionSpec as P

HD = 128
PAGE = 8
TOK = 512
MESH = pl.DeviceIdType.MESH

rope_theta = 500000.0
neg_large = -1e30


def kernel(
    hidden, w_query, w_key, w_value, cosine, sine, page_src, source_of, flag,
    attended, kv_cache,
    W, hid, acc, ks, vs, qs, att, pg, p1, p2, p3, p4, m0, r0, m1, r1, m2, r2, r3, r4, kvo,
    loc, send, rec_a, rec_b, rec_c, line_s, line_r, page_s, page_r, page_l, anc_s, anc_r, out_s,
):
    c = lax.axis_index("ctx")
    x = c // 16
    y = (c // 4) % 4
    z = c % 4
    coords = {"x": x, "y": y, "z": z}

    def peer(axis, i):
        if axis == "x":
            return {"ctx": i * 16 + y * 4 + z}
        if axis == "y":
            return {"ctx": x * 16 + i * 4 + z}
        return {"ctx": x * 16 + y * 4 + i}

    def remote(src, dst, s, r, axis, i):
        pltpu.make_async_remote_copy(
            src_ref=src, dst_ref=dst, send_sem=s, recv_sem=r,
            device_id=peer(axis, i), device_id_type=MESH,
        ).start()

    def wait(ref, sem):
        pltpu.make_async_copy(ref, ref, sem).wait()

    def own_copy(g):
        if g == 0:
            src = w_key
        elif g == 1:
            src = w_value
        else:
            src = w_query.at[:, pl.ds((g - 2) * HD, HD)]
        return pltpu.make_async_copy(src, W.at[g, x, y, z], loc.at[g])

    hid_copies = [
        pltpu.make_async_copy(hidden.at[:, pl.ds(i * 2048, 2048)], hid.at[i], loc.at[10 + i])
        for i in range(4)
    ]
    for g in (0, 1, 8, 9, 2, 3, 4, 5, 6, 7):
        own_copy(g).start()

    barrier = pltpu.get_barrier_semaphore()
    for axis in "xyz":
        for d in (1, 2, 3):
            pl.semaphore_signal(
                barrier, inc=1, device_id=peer(axis, (coords[axis] + d) % 4), device_id_type=MESH
            )
    pl.semaphore_wait(barrier, 9)

    def first_axis(g):
        return "x" if g >= 8 else "z"

    def a_start(g):
        own_copy(g).wait()
        axis = first_axis(g)
        mine = W.at[g, x, y, z]
        for d in (1, 3, 2):
            remote(mine, mine, send.at[g, 0], rec_a.at[g], axis, (coords[axis] + d) % 4)

    def a_wait(g):
        wait(W.at[g, x, y, 0:3], rec_a.at[g])

    def layout(g, phase):
        if g >= 8:
            return "y", lambda i, h: W.at[g, pl.ds(2 * h, 2), i, z], lambda n: W.at[g, :, 0:n, z]
        if g % 2 == 0:
            if phase == 1:
                return "y", lambda i, h: W.at[g, x, i, pl.ds(2 * h, 2)], lambda n: W.at[g, x, 0:n]
            return "x", lambda i, h: W.at[g, i, pl.ds(2 * h, 2)], lambda n: W.at[g, 0:n]
        if phase == 1:
            return "x", lambda i, h: W.at[g, i, y, pl.ds(2 * h, 2)], lambda n: W.at[g, 0:n, y]
        return "y", lambda i, h: W.at[g, pl.ds(2 * h, 2), i], lambda n: W.at[g, :, 0:n]

    def rec(g, phase):
        return rec_b.at[g] if phase == 1 else rec_c.at[g]

    def ring_start(g, phase):
        axis, slab, _ = layout(g, phase)
        i = coords[axis]
        right, left = (i + 1) % 4, (i + 3) % 4
        s, r = send.at[g, phase], rec(g, phase)
        remote(slab(i, 0), slab(i, 0), s, r.at[0], axis, right)
        remote(slab(i, 1), slab(i, 1), s, r.at[1], axis, left)
        remote(slab(i, 1), slab(i, 1), s, r.at[2], axis, right)
        remote(slab(i, 0), slab(i, 0), s, r.at[2], axis, left)

    def ring_pass(g, phase):
        axis, slab, _ = layout(g, phase)
        i = coords[axis]
        right, left = (i + 1) % 4, (i + 3) % 4
        s, r = send.at[g, phase], rec(g, phase)
        wait(slab(left, 0), r.at[0])
        remote(slab(left, 0), slab(left, 0), s, r.at[2], axis, right)
        wait(slab(right, 1), r.at[1])
        remote(slab(right, 1), slab(right, 1), s, r.at[2], axis, left)

    def ring_wait(g, phase):
        wait(layout(g, phase)[2](2), rec(g, phase).at[2])

    b_start, b_pass, b_wait = (functools.partial(f, phase=1) for f in (ring_start, ring_pass, ring_wait))
    c_start, c_pass, c_wait = (functools.partial(f, phase=2) for f in (ring_start, ring_pass, ring_wait))

    def line_send(g, step, up):
        slab = W.at[g, :, :, z - step if up else z + step]
        k = step * 2 + (0 if up else 1)
        return pltpu.make_async_remote_copy(
            src_ref=slab, dst_ref=slab, send_sem=line_s.at[g - 8, k], recv_sem=line_r.at[g - 8, k],
            device_id=peer("z", z + 1 if up else z - 1), device_id_type=MESH,
        )

    def sends_up(step):
        return (z >= step) & (z < 3)

    def sends_down(step):
        return (z <= 3 - step) & (z > 0)

    def line_step(g, step):
        if step > 0:
            line_take(g, step - 1)
        if step < 3:
            @pl.when(sends_up(step))
            def _():
                line_send(g, step, True).start()

            @pl.when(sends_down(step))
            def _():
                line_send(g, step, False).start()

    def line_take(g, step):
        @pl.when(z >= step + 1)
        def _():
            wait(W.at[g, :, :, z - step - 1], line_r.at[g - 8, step * 2])

        @pl.when(z <= 2 - step)
        def _():
            wait(W.at[g, :, :, z + step + 1], line_r.at[g - 8, step * 2 + 1])

    def project(g0, g1):
        acc[...] = jnp.zeros_like(acc)

        def step(i, carry):
            w = jnp.concatenate(
                [W[g0, i].reshape(2048, HD), W[g1, i].reshape(2048, HD)], axis=1
            )
            acc[...] += jnp.dot(hid[i], w, preferred_element_type=jnp.float32)
            return carry

        lax.fori_loop(0, 4, step, 0)

    def rotated(v):
        return v * cosine[...] + pltpu.roll(v, HD // 2, 1) * sine[...]

    def queries(g0, g1):
        project(g0, g1)
        qs[g0 - 2] = rotated(acc[:, :HD]).astype(jnp.bfloat16)
        qs[g1 - 2] = rotated(acc[:, HD:]).astype(jnp.bfloat16)

    factor = math.log2(math.e) / math.sqrt(HD)
    last = (((1,), (1,)), ((), ()))

    def attend(g0):
        far_bias = flag[0] * neg_large

        def one(k, carry):
            h = g0 - 2 + k
            far_key = r4[0:2].reshape(TOK, HD)
            far_value = r4[2:4].reshape(TOK, HD)
            for b in range(2):
                n = 256 * (b + 1)
                q = qs[h, b * 256:n, :]
                own = lax.dot_general(q, ks[0:n, :], last, preferred_element_type=jnp.float32)
                rows = lax.broadcasted_iota(jnp.int32, (256, n), 0) + b * 256
                columns = lax.broadcasted_iota(jnp.int32, (256, n), 1)
                own = jnp.where(rows >= columns, own, neg_large)
                far = lax.dot_general(q, far_key, last, preferred_element_type=jnp.float32)
                far = far + far_bias
                top = jnp.maximum(
                    jnp.max(own, -1, keepdims=True), jnp.max(far, -1, keepdims=True)
                )
                own = jnp.exp2((own - top) * factor)
                far = jnp.exp2((far - top) * factor)
                total = jnp.sum(own, -1, keepdims=True) + jnp.sum(far, -1, keepdims=True)
                scale = 1.0 / total
                result = jnp.dot(
                    (own * scale).astype(jnp.bfloat16), vs[0:n, :],
                    preferred_element_type=jnp.float32,
                )
                result += jnp.dot(
                    (far * scale).astype(jnp.bfloat16), far_value,
                    preferred_element_type=jnp.float32,
                )
                att[h, b * 256:n, :] = result.astype(jnp.bfloat16)
            return carry

        lax.fori_loop(0, 2, one, 0)
        for h in (g0 - 2, g0 - 1):
            out_copy(h).start()

    def out_copy(h):
        return pltpu.make_async_copy(att.at[h], attended.at[:, pl.ds(h * HD, HD)], out_s.at[h])

    def page_own(step):
        if step == 0:
            return pltpu.make_async_copy(p1.at[x], p2.at[x], page_l.at[0])
        if step == 1:
            return pltpu.make_async_copy(p2.at[:, y], p3.at[pl.ds(y * 4, 4)], page_l.at[1])
        return pltpu.make_async_copy(p3.at[:, z], p4.at[pl.ds(z * 16, 16)], page_l.at[2])

    def page_start(step):
        axis = "xyz"[step]
        page_own(step).start()
        for d in (1, 3, 2):
            i = (coords[axis] + d) % 4
            if step == 0:
                src, dst = p1.at[i], p2.at[x]
            elif step == 1:
                src, dst = p2.at[:, i], p3.at[pl.ds(y * 4, 4)]
            else:
                src, dst = p3.at[:, i], p4.at[pl.ds(z * 16, 16)]
            remote(src, dst, page_s.at[step], page_r.at[step], axis, i)

    def page_wait(step, sem):
        wait((p2.at[0:3], p3.at[0:12], p4.at[0:48])[step], sem.at[step])

    def page_take(step):
        page_own(step).wait()
        page_wait(step, page_r)

    anchor_steps = (
        ("x", m0, r0), ("y", m1, r1), ("z", None, r2), ("y", None, r3), ("x", None, r4),
    )

    def anchor_start(step):
        axis, parts, to = anchor_steps[step]
        i = coords[axis]
        if step == 0:
            r0[x] = m0[x]
        elif step == 1:
            total = r0[0] + r0[1] + r0[2] + r0[3]
            m1[...] = total.reshape(4, 64, HD)
            r1[y] = m1[y]
        elif step == 2:
            m2[...] = r1[0] + r1[1] + r1[2] + r1[3]
            r2[z] = m2[...]
        elif step == 3:
            r3[y] = r2[0] + r2[1] + r2[2] + r2[3]
        else:
            r4[x] = r3[...].reshape(256, HD)
        for d in (1, 3, 2):
            j = (i + d) % 4
            src = parts.at[j] if parts is not None else to.at[i]
            remote(src, to.at[i], anc_s.at[step], anc_r.at[step], axis, j)

    def anchor_wait(step, sem):
        wait(anchor_steps[step][2].at[0:3], sem.at[step])

    def anchor_take(step):
        anchor_wait(step, anc_r)

    def keys_values():
        project(0, 1)
        key = rotated(acc[:, :HD]).astype(jnp.bfloat16)
        value = acc[:, HD:].astype(jnp.bfloat16)
        ks[...] = key
        vs[...] = value
        root = flag[0]
        wide_key, wide_value = key.astype(jnp.float32), value.astype(jnp.float32)
        m0[0:2] = (wide_key * root).astype(jnp.bfloat16).reshape(2, 256, HD)
        m0[2:4] = (wide_value * root).astype(jnp.bfloat16).reshape(2, 256, HD)
        pg[0:64, :, 0:HD] = wide_key.reshape(64, PAGE, HD)
        pg[0:64, :, HD:2 * HD] = wide_value.reshape(64, PAGE, HD)
        pg[64] = jnp.zeros((PAGE, 2 * HD), jnp.float32)

    def deal_pages():
        def one(o, carry):
            pair = jnp.concatenate([pg[page_src[2 * o]], pg[page_src[2 * o + 1]]], axis=0)
            p1[o // 16, (o // 4) % 4, o % 4] = pair.astype(jnp.bfloat16)
            return carry

        lax.fori_loop(0, 64, one, 0)

    def place_pages():
        def one(b, carry):
            kvo[b] = p4[source_of[b]]
            return carry

        lax.fori_loop(0, 64, one, 0)

    kv_copy = pltpu.make_async_copy(kvo, kv_cache, out_s.at[8])

    def each(f, *groups):
        for g in groups:
            f(g)

    each(a_start, 0, 1, 8, 9, 2, 3)
    for copy in hid_copies:
        copy.start()
    for g in (0, 1, 8, 9):
        a_wait(g)
        b_start(g)
    each(b_pass, 0, 1)
    for g in (0, 1):
        b_wait(g)
        c_start(g)
    b_pass(8)
    b_wait(8)
    line_step(8, 0)
    for g in (2, 3):
        a_wait(g)
        b_start(g)
    b_pass(9)
    b_wait(9)
    each(a_start, 4, 5)
    each(c_pass, 0, 1)
    each(b_pass, 2, 3)
    line_step(8, 1)
    line_step(9, 0)
    for g in (2, 3):
        b_wait(g)
        c_start(g)
    each(c_wait, 0, 1)
    for copy in hid_copies:
        copy.wait()
    keys_values()
    anchor_start(0)
    deal_pages()
    page_start(0)
    for g in (4, 5):
        a_wait(g)
        b_start(g)
    each(a_start, 6, 7)
    anchor_take(0)
    anchor_start(1)
    each(c_pass, 2, 3)
    line_step(8, 2)
    page_take(0)
    page_start(1)
    anchor_take(1)
    anchor_start(2)
    each(b_pass, 4, 5)
    for g in (4, 5):
        b_wait(g)
        c_start(g)
    page_take(1)
    page_start(2)
    anchor_take(2)
    anchor_start(3)
    each(c_wait, 2, 3)
    queries(2, 3)
    anchor_take(3)
    anchor_start(4)
    line_step(9, 1)
    for g in (6, 7):
        a_wait(g)
        b_start(g)
    each(c_pass, 4, 5)
    line_step(8, 3)
    anchor_take(4)
    each(b_pass, 6, 7)
    for g in (6, 7):
        b_wait(g)
        c_start(g)
    attend(2)
    line_step(9, 2)
    each(c_wait, 4, 5)
    queries(4, 5)
    each(c_pass, 6, 7)
    attend(4)
    page_take(2)
    place_pages()
    kv_copy.start()
    line_step(9, 3)
    queries(8, 9)
    attend(8)
    each(c_wait, 6, 7)
    queries(6, 7)
    attend(6)

    for g in range(10):
        wait(W.at[g, 0, 0, 0:3], send.at[g, 0])
        wait(layout(g, 1)[2](3), send.at[g, 1])
        if g < 8:
            wait(layout(g, 2)[2](3), send.at[g, 2])
    for g in (8, 9):
        for step in range(3):
            @pl.when(sends_up(step))
            def _():
                line_send(g, step, True).wait_send()

            @pl.when(sends_down(step))
            def _():
                line_send(g, step, False).wait_send()
    for step in range(3):
        page_wait(step, page_s)
    for step in range(5):
        anchor_wait(step, anc_s)
    for h in range(8):
        out_copy(h).wait()
    kv_copy.wait()


def on_device(hidden, w_query, w_key, w_value, block_order, page_map):
    ctx_count = lax.axis_size("ctx")
    my_block = block_order[lax.axis_index("ctx")]
    half = HD // 2
    exponent = jnp.arange(half, dtype=jnp.float32) * (2.0 / HD)
    inverse = jnp.exp(-exponent * jnp.log(jnp.float32(rope_theta)))
    positions = (my_block * TOK + jnp.arange(TOK, dtype=jnp.int32)).astype(jnp.float32)
    angles = positions[:, None] * inverse[None, :]
    cosine, sine = jnp.cos(angles), jnp.sin(angles)
    cosine = jnp.concatenate([cosine, cosine], -1)
    sine = jnp.concatenate([-sine, sine], -1)

    pages = TOK // PAGE
    owners = lax.dynamic_slice_in_dim(page_map[:, 0], my_block * pages, pages, 0)
    number = jnp.arange(pages, dtype=jnp.int32)
    same = owners[:, None] == owners[None, :]
    rank = jnp.sum((same & (number[None, :] < number[:, None])).astype(jnp.int32), -1)
    slot = owners * 2 + rank
    match = slot[None, :] == jnp.arange(2 * ctx_count, dtype=jnp.int32)[:, None]
    page_src = pages + jnp.sum(jnp.where(match, number[None, :] - pages, 0), -1)
    where = jnp.arange(ctx_count, dtype=jnp.int32)
    arrived = (where % 4) * 16 + ((where // 4) % 4) * 4 + where // 16
    source_of = jnp.sum(
        jnp.where(block_order[None, :] == where[:, None], arrived[None, :], 0), -1
    )
    flag = (my_block == 0).astype(jnp.float32).reshape(1)

    hbm = pl.BlockSpec(memory_space=pl.ANY)
    vmem = pl.BlockSpec(memory_space=pltpu.VMEM)
    smem = pl.BlockSpec(memory_space=pltpu.SMEM)
    bf16, f32, dma = jnp.bfloat16, jnp.float32, pltpu.SemaphoreType.DMA
    attended, kv = pl.pallas_call(
        kernel,
        out_shape=(
            jax.ShapeDtypeStruct((TOK, 8 * HD), bf16),
            jax.ShapeDtypeStruct((64, 16, 2 * HD), bf16),
        ),
        in_specs=[hbm] * 4 + [vmem] * 2 + [smem] * 3,
        out_specs=(hbm, hbm),
        scratch_shapes=[
            pltpu.VMEM((10, 4, 4, 4, 128, 128), bf16),
            pltpu.VMEM((4, TOK, 2048), bf16),
            pltpu.VMEM((TOK, 256), f32),
            pltpu.VMEM((TOK, HD), bf16),
            pltpu.VMEM((TOK, HD), bf16),
            pltpu.VMEM((8, TOK, HD), bf16),
            pltpu.VMEM((8, TOK, HD), bf16),
            pltpu.VMEM((65, PAGE, 2 * HD), f32),
            pltpu.VMEM((4, 4, 4, 16, 2 * HD), bf16),
            pltpu.VMEM((4, 4, 4, 16, 2 * HD), bf16),
            pltpu.VMEM((16, 4, 16, 2 * HD), bf16),
            pltpu.VMEM((64, 16, 2 * HD), bf16),
            pltpu.VMEM((4, 256, HD), bf16),
            pltpu.VMEM((4, 256, HD), bf16),
            pltpu.VMEM((4, 64, HD), bf16),
            pltpu.VMEM((4, 64, HD), bf16),
            pltpu.VMEM((64, HD), bf16),
            pltpu.VMEM((4, 64, HD), bf16),
            pltpu.VMEM((4, 64, HD), bf16),
            pltpu.VMEM((4, 256, HD), bf16),
            pltpu.VMEM((64, 16, 2 * HD), bf16),
            dma((14,)),
            dma((10, 3)),
            dma((10,)),
            dma((10, 3)),
            dma((8, 3)),
            dma((2, 6)),
            dma((2, 6)),
            dma((3,)),
            dma((3,)),
            dma((3,)),
            dma((5,)),
            dma((5,)),
            dma((9,)),
        ],
        compiler_params=pltpu.CompilerParams(
            collective_id=0, has_side_effects=True, vmem_limit_bytes=56 * 1024 * 1024
        ),
        cost_estimate=pl.CostEstimate(
            flops=2 * TOK * 8192 * 1280, bytes_accessed=12 << 20, transcendentals=8 * TOK * 1024
        ),
    )(hidden, w_query, w_key, w_value, cosine, sine, page_src, source_of, flag)
    return attended, kv.reshape(1, ctx_count, 2, PAGE, 2 * HD)


def solution(mesh):
    placed = (P("ctx", None), P("ctx", "tp"), P("ctx", "tp"), P("ctx", "tp"), P(), P())
    return jax.shard_map(
        on_device,
        mesh=mesh,
        in_specs=placed,
        out_specs=(P("ctx", "tp"), P("ctx", None, None, None, "tp")),
        check_vma=False,
    )
```

```python
import functools
import math

import jax
import jax.numpy as jnp
from jax import lax
from jax.experimental import pallas as pl
from jax.experimental.pallas import tpu as pltpu
from jax.sharding import PartitionSpec as P

HD = 128
PAGE = 8
TOK = 512
MESH = pl.DeviceIdType.MESH

rope_theta = 500000.0
neg_large = -1e30


def kernel(
    hidden, w_query, w_key, w_value, cosine, sine, page_src, source_of, flag,
    attended, kv_cache,
    wkv, wq, hid, hid_p, acc, q_own, part_s, part_r,
    kt, vs, qs, att, pg, p1, p2, p3, p4, m0, r0, m1, r1, r2, r3, r4, kvo,
    loc, hid_l, send, rec_a, rec_b, rec_c, hid_s, hid_r, core_s, core_r, par_s, par_r,
    page_s, page_r, page_l, anc_s, anc_r, out_s,
):
    c = lax.axis_index("ctx")
    x = c // 16
    y = (c // 4) % 4
    z = c % 4
    half, parity = z // 2, z % 2
    beside = z + 1 - 2 * parity
    tp = lax.axis_index("tp")
    core = tp % 2
    coords = {"x": x, "y": y, "z": z}

    def peer(axis, i):
        if axis == "x":
            return {"ctx": i * 16 + y * 4 + z}
        if axis == "y":
            return {"ctx": x * 16 + i * 4 + z}
        return {"ctx": x * 16 + y * 4 + i}

    def remote(src, dst, s, r, axis, i):
        pltpu.make_async_remote_copy(
            src_ref=src, dst_ref=dst, send_sem=s, recv_sem=r,
            device_id=peer(axis, i), device_id_type=MESH,
        ).start()

    def wait(ref, sem):
        pltpu.make_async_copy(ref, ref, sem).wait()

    def mine(g):
        return wkv.at[g, x, y, z] if g < 2 else wq.at[g - 2, x, y, half]

    def own_copy(g):
        if g == 0:
            src = w_key
        elif g == 1:
            src = w_value
        else:
            src = w_query.at[:, pl.ds((g - 2) * HD, HD)]
        return pltpu.make_async_copy(src, mine(g), loc.at[g])

    for g in range(10):
        own_copy(g).start()

    def hid_load(k, carry):
        pltpu.make_async_copy(
            hidden.at[:, pl.ds(pl.multiple_of(k * HD, HD), HD)],
            hid.at[k // 16, (k // 4) % 4, (k // 2) % 2, k % 2],
            hid_l.at[0],
        ).start()
        return carry

    lax.fori_loop(0, 64, hid_load, 0)

    barrier = pltpu.get_barrier_semaphore()
    for axis in "xyz":
        for d in (1, 2, 3):
            pl.semaphore_signal(
                barrier, inc=1, device_id=peer(axis, (coords[axis] + d) % 4), device_id_type=MESH
            )
    pl.semaphore_signal(
        barrier, inc=1, device_id={"tp": tp + 1 - 2 * core}, device_id_type=MESH
    )
    pl.semaphore_wait(barrier, 10)

    def a_start(g):
        own_copy(g).wait()
        if g < 2:
            for d in (1, 3, 2):
                remote(mine(g), mine(g), send.at[g, 0], rec_a.at[g], "z", (z + d) % 4)
        else:
            remote(mine(g), mine(g), send.at[g, 0], rec_a.at[g], "z", (z + 2) % 4)

    def a_done(g, sem):
        wait(wkv.at[g, x, y, 0:3] if g < 2 else wq.at[g - 2, x, y, 0], sem)

    def a_wait(g):
        a_done(g, rec_a.at[g])

    def layout(g, phase):
        w, k, n_half = (wkv, g, 2) if g < 2 else (wq, g - 2, 1)
        if g % 2 == 0:
            if phase == 1:
                return (
                    "y",
                    lambda i, h: w.at[k, x, i, pl.ds(n_half * h, n_half)],
                    lambda n: w.at[k, x, 0:n],
                )
            return "x", lambda i, h: w.at[k, i, pl.ds(2 * h, 2)], lambda n: w.at[k, 0:n]
        if phase == 1:
            return (
                "x",
                lambda i, h: w.at[k, i, y, pl.ds(n_half * h, n_half)],
                lambda n: w.at[k, 0:n, y],
            )
        return "y", lambda i, h: w.at[k, pl.ds(2 * h, 2), i], lambda n: w.at[k, :, 0:n]

    def rec(g, phase):
        return rec_b.at[g] if phase == 1 else rec_c.at[g]

    def ring_start(g, phase):
        axis, slab, _ = layout(g, phase)
        i = coords[axis]
        right, left = (i + 1) % 4, (i + 3) % 4
        s, r = send.at[g, phase], rec(g, phase)
        remote(slab(i, 0), slab(i, 0), s, r.at[0], axis, right)
        remote(slab(i, 1), slab(i, 1), s, r.at[1], axis, left)
        remote(slab(i, 1), slab(i, 1), s, r.at[2], axis, right)
        remote(slab(i, 0), slab(i, 0), s, r.at[2], axis, left)

    def ring_pass(g, phase):
        axis, slab, _ = layout(g, phase)
        i = coords[axis]
        right, left = (i + 1) % 4, (i + 3) % 4
        s, r = send.at[g, phase], rec(g, phase)
        wait(slab(left, 0), r.at[0])
        remote(slab(left, 0), slab(left, 0), s, r.at[2], axis, right)
        wait(slab(right, 1), r.at[1])
        remote(slab(right, 1), slab(right, 1), s, r.at[2], axis, left)

    def ring_wait(g, phase):
        wait(layout(g, phase)[2](2), rec(g, phase).at[2])

    b_start, b_pass, b_wait = (functools.partial(f, phase=1) for f in (ring_start, ring_pass, ring_wait))
    c_start, c_pass, c_wait = (functools.partial(f, phase=2) for f in (ring_start, ring_pass, ring_wait))

    def hid_piece(ref, k):
        return ref.at[k // 2, pl.ds(2 * (k % 2), 2)]

    def hid_start(j):
        k = core * 4 + j
        remote(
            hid.at[k // 2, pl.ds(2 * (k % 2), 2), :, 1 - parity], hid_piece(hid_p, k),
            hid_s.at[0], hid_r.at[j], "z", beside,
        )

    def hid_pass(j):
        k = core * 4 + j
        piece = hid_piece(hid_p, k)
        wait(piece, hid_r.at[j])
        pltpu.make_async_remote_copy(
            src_ref=piece, dst_ref=piece, send_sem=core_s.at[0], recv_sem=core_r.at[0],
            device_id={"tp": tp + 1 - 2 * core}, device_id_type=MESH,
        ).start()

    def project(left_of, k, w, pieces):
        rows = pieces * HD
        total = None
        for i in range(4):
            right = jnp.concatenate(
                [w[k, i].reshape(rows, HD), w[k + 1, i].reshape(rows, HD)], axis=1
            )
            d = jnp.dot(left_of(i), right, preferred_element_type=jnp.float32)
            total = d if total is None else total + d
        acc[...] = total

    def all_hidden(i):
        return jnp.concatenate(
            [hid[i, b, e, f] for b in range(4) for e in range(2) for f in range(2)], axis=1
        )

    def own_hidden(i):
        return jnp.concatenate(
            [hid[i, b, e, parity] for b in range(4) for e in range(2)], axis=1
        )

    def other_hidden(i):
        return jnp.concatenate([hid_p[i, b, e] for b in range(4) for e in range(2)], axis=1)

    def rotated(v):
        return v * cosine[...] + pltpu.roll(v, HD // 2, 1) * sine[...]

    def parts_other(g):
        h = g - 2
        project(other_hidden, h, wq, 8)
        part_s[h] = acc[:, :HD].astype(jnp.bfloat16)
        part_s[h + 1] = acc[:, HD:].astype(jnp.bfloat16)
        pair = pl.ds(h, 2)
        remote(part_s.at[pair], part_r.at[pair], par_s.at[h // 2], par_r.at[h // 2], "z", beside)

    def parts_own(g):
        h = g - 2
        project(own_hidden, h, wq, 8)
        q_own[h] = acc[:, :HD]
        q_own[h + 1] = acc[:, HD:]

    def part_wait(h, sem):
        wait(part_r.at[pl.ds(h, 2)], sem.at[h // 2])

    def queries(g):
        part_wait(g - 2, par_r)
        for h in (g - 2, g - 1):
            qs[h] = rotated(q_own[h] + part_r[h].astype(jnp.float32)).astype(jnp.bfloat16)

    factor = math.log2(math.e) / math.sqrt(HD)

    def anchor_ready():
        kt[:, 0:TOK] = r4[0:2].reshape(TOK, HD).astype(jnp.float32).T.astype(jnp.bfloat16)
        vs[0:TOK, 0:HD] = r4[2:4].reshape(TOK, HD)
        vs[:, HD:] = jnp.ones((2 * TOK, HD), jnp.bfloat16)

    def attend(g0):
        far_bias = flag[0] * neg_large

        def one(k, carry):
            h = g0 - 2 + k
            for b in range(2):
                n = 768 + 256 * b
                q = qs[h, b * 256:b * 256 + 256, :]
                scores = jnp.dot(q, kt[:, 0:n], preferred_element_type=jnp.float32)
                rows = lax.broadcasted_iota(jnp.int32, (256, 256), 0)
                columns = lax.broadcasted_iota(jnp.int32, (256, 256), 1)
                last = jnp.where(rows >= columns, scores[:, n - 256:], neg_large)
                far = scores[:, 0:TOK] + far_bias
                pieces = [far, last] if b == 0 else [far, scores[:, TOK:n - 256], last]
                top = functools.reduce(
                    jnp.maximum, [jnp.max(v, -1, keepdims=True) for v in pieces]
                )
                weights = jnp.concatenate(
                    [jnp.exp2((v - top) * factor).astype(jnp.bfloat16) for v in pieces], axis=1
                )
                result = jnp.dot(weights, vs[0:n, :], preferred_element_type=jnp.float32)
                att[h, b * 256:b * 256 + 256, :] = (
                    result[:, 0:HD] / result[:, HD:]
                ).astype(jnp.bfloat16)
            return carry

        one(0, 0)
        one(1, 0)
        for h in (g0 - 2, g0 - 1):
            out_copy(h).start()

    def out_copy(h):
        return pltpu.make_async_copy(att.at[h], attended.at[:, pl.ds(h * HD, HD)], out_s.at[h])

    def page_own(step):
        if step == 0:
            return pltpu.make_async_copy(p1.at[x], p2.at[x], page_l.at[0])
        if step == 1:
            return pltpu.make_async_copy(p2.at[:, y], p3.at[pl.ds(y * 4, 4)], page_l.at[1])
        return pltpu.make_async_copy(p3.at[:, z], p4.at[pl.ds(z * 16, 16)], page_l.at[2])

    def page_start(step):
        axis = "xyz"[step]
        page_own(step).start()
        for d in (1, 3, 2):
            i = (coords[axis] + d) % 4
            if step == 0:
                src, dst = p1.at[i], p2.at[x]
            elif step == 1:
                src, dst = p2.at[:, i], p3.at[pl.ds(y * 4, 4)]
            else:
                src, dst = p3.at[:, i], p4.at[pl.ds(z * 16, 16)]
            remote(src, dst, page_s.at[step], page_r.at[step], axis, i)

    def page_wait(step, sem):
        wait((p2.at[0:3], p3.at[0:12], p4.at[0:48])[step], sem.at[step])

    def page_take(step):
        page_own(step).wait()
        page_wait(step, page_r)

    anchor_steps = (
        ("x", m0, r0), ("y", m1, r1), ("z", None, r2), ("y", None, r3), ("x", None, r4),
    )

    def anchor_start(step):
        axis, parts, to = anchor_steps[step]
        i = coords[axis]
        if step == 0:
            r0[x] = m0[x]
        elif step == 1:
            total = r0[0] + r0[1] + r0[2] + r0[3]
            m1[...] = total.reshape(4, 64, HD)
            r1[y] = m1[y]
        elif step == 2:
            r2[z] = r1[0] + r1[1] + r1[2] + r1[3]
        elif step == 3:
            r3[y] = r2[0] + r2[1] + r2[2] + r2[3]
        else:
            r4[x] = r3[...].reshape(256, HD)
        for d in (1, 3, 2):
            j = (i + d) % 4
            src = parts.at[j] if parts is not None else to.at[i]
            remote(src, to.at[i], anc_s.at[step], anc_r.at[step], axis, j)

    def anchor_wait(step, sem):
        wait(anchor_steps[step][2].at[0:3], sem.at[step])

    def anchor_take(step):
        anchor_wait(step, anc_r)

    def keys_values():
        project(all_hidden, 0, wkv, 16)
        key = rotated(acc[:, :HD]).astype(jnp.bfloat16)
        value = acc[:, HD:].astype(jnp.bfloat16)
        root = flag[0]
        wide_key, wide_value = key.astype(jnp.float32), value.astype(jnp.float32)
        kt[:, TOK:] = wide_key.T.astype(jnp.bfloat16)
        vs[TOK:, 0:HD] = value
        m0[0:2] = (wide_key * root).astype(jnp.bfloat16).reshape(2, 256, HD)
        m0[2:4] = (wide_value * root).astype(jnp.bfloat16).reshape(2, 256, HD)
        pg[0:64, :, 0:HD] = wide_key.reshape(64, PAGE, HD)
        pg[0:64, :, HD:2 * HD] = wide_value.reshape(64, PAGE, HD)
        pg[64] = jnp.zeros((PAGE, 2 * HD), jnp.float32)

    def deal_pages():
        def one(o, carry):
            pair = jnp.concatenate([pg[page_src[2 * o]], pg[page_src[2 * o + 1]]], axis=0)
            p1[o // 16, (o // 4) % 4, o % 4] = pair.astype(jnp.bfloat16)
            return carry

        lax.fori_loop(0, 64, one, 0)

    def place_pages():
        def one(b, carry):
            kvo[b] = p4[source_of[b]]
            return carry

        lax.fori_loop(0, 64, one, 0)

    kv_copy = pltpu.make_async_copy(kvo, kv_cache, out_s.at[8])

    def each(f, *groups):
        for g in groups:
            f(g)

    each(a_start, 0, 1)
    for g in (0, 1):
        a_wait(g)
        b_start(g)
    each(a_start, *range(2, 10))
    wait(hid, hid_l.at[0])
    each(hid_start, 0, 1, 2, 3)
    each(b_pass, 0, 1)
    for g in (0, 1):
        b_wait(g)
        c_start(g)
    for g in (2, 3):
        a_wait(g)
        b_start(g)
    each(c_pass, 0, 1)
    for g in (4, 5):
        a_wait(g)
        b_start(g)
    each(b_pass, 2, 3)
    for g in (2, 3):
        b_wait(g)
        c_start(g)
    each(b_pass, 4, 5)
    hid_pass(0)
    each(c_wait, 0, 1)
    keys_values()
    anchor_start(0)
    each(c_pass, 2, 3)
    for g in (6, 7):
        a_wait(g)
        b_start(g)
    deal_pages()
    page_start(0)
    for g in (4, 5):
        b_wait(g)
        c_start(g)
    hid_pass(1)
    each(b_pass, 6, 7)
    anchor_take(0)
    anchor_start(1)
    each(c_wait, 2, 3)
    parts_own(2)
    each(c_pass, 4, 5)
    for g in (8, 9):
        a_wait(g)
        b_start(g)
    hid_pass(2)
    page_take(0)
    page_start(1)
    anchor_take(1)
    anchor_start(2)
    for g in (6, 7):
        b_wait(g)
        c_start(g)
    each(b_pass, 8, 9)
    anchor_take(2)
    anchor_start(3)
    hid_pass(3)
    each(c_wait, 4, 5)
    each(c_pass, 6, 7)
    parts_own(4)
    for g in (8, 9):
        b_wait(g)
        c_start(g)
    anchor_take(3)
    anchor_start(4)
    wait(hid_p.at[0:2], core_r.at[0])
    parts_other(2)
    parts_other(4)
    page_take(1)
    page_start(2)
    each(c_wait, 6, 7)
    parts_other(6)
    each(c_pass, 8, 9)
    parts_own(6)
    anchor_take(4)
    anchor_ready()
    queries(2)
    attend(2)
    queries(4)
    attend(4)
    each(c_wait, 8, 9)
    parts_other(8)
    parts_own(8)
    queries(6)
    attend(6)
    page_take(2)
    place_pages()
    kv_copy.start()
    queries(8)
    attend(8)

    for g in range(10):
        a_done(g, send.at[g, 0])
        wait(layout(g, 1)[2](3), send.at[g, 1])
        wait(layout(g, 2)[2](3), send.at[g, 2])
    wait(hid_p.at[0:2], hid_s.at[0])
    wait(hid_p.at[0:2], core_s.at[0])
    for h in (0, 2, 4, 6):
        part_wait(h, par_s)
    for step in range(3):
        page_wait(step, page_s)
    for step in range(5):
        anchor_wait(step, anc_s)
    for h in range(8):
        out_copy(h).wait()
    kv_copy.wait()


def on_device(hidden, w_query, w_key, w_value, block_order, page_map):
    ctx_count = lax.axis_size("ctx")
    my_block = block_order[lax.axis_index("ctx")]
    half = HD // 2
    exponent = jnp.arange(half, dtype=jnp.float32) * (2.0 / HD)
    inverse = jnp.exp(-exponent * jnp.log(jnp.float32(rope_theta)))
    positions = (my_block * TOK + jnp.arange(TOK, dtype=jnp.int32)).astype(jnp.float32)
    angles = positions[:, None] * inverse[None, :]
    cosine, sine = jnp.cos(angles), jnp.sin(angles)
    cosine = jnp.concatenate([cosine, cosine], -1)
    sine = jnp.concatenate([-sine, sine], -1)

    pages = TOK // PAGE
    owners = lax.dynamic_slice_in_dim(page_map[:, 0], my_block * pages, pages, 0)
    number = jnp.arange(pages, dtype=jnp.int32)
    same = owners[:, None] == owners[None, :]
    rank = jnp.sum((same & (number[None, :] < number[:, None])).astype(jnp.int32), -1)
    slot = owners * 2 + rank
    match = slot[None, :] == jnp.arange(2 * ctx_count, dtype=jnp.int32)[:, None]
    page_src = pages + jnp.sum(jnp.where(match, number[None, :] - pages, 0), -1)
    where = jnp.arange(ctx_count, dtype=jnp.int32)
    arrived = (where % 4) * 16 + ((where // 4) % 4) * 4 + where // 16
    source_of = jnp.sum(
        jnp.where(block_order[None, :] == where[:, None], arrived[None, :], 0), -1
    )
    flag = (my_block == 0).astype(jnp.float32).reshape(1)

    hbm = pl.BlockSpec(memory_space=pl.ANY)
    vmem = pl.BlockSpec(memory_space=pltpu.VMEM)
    smem = pl.BlockSpec(memory_space=pltpu.SMEM)
    bf16, f32, dma = jnp.bfloat16, jnp.float32, pltpu.SemaphoreType.DMA
    attended, kv = pl.pallas_call(
        kernel,
        out_shape=(
            jax.ShapeDtypeStruct((TOK, 8 * HD), bf16),
            jax.ShapeDtypeStruct((64, 16, 2 * HD), bf16),
        ),
        in_specs=[hbm] * 4 + [vmem] * 2 + [smem] * 3,
        out_specs=(hbm, hbm),
        scratch_shapes=[
            pltpu.VMEM((2, 4, 4, 4, HD, HD), bf16),
            pltpu.VMEM((8, 4, 4, 2, HD, HD), bf16),
            pltpu.VMEM((4, 4, 2, 2, TOK, HD), bf16),
            pltpu.VMEM((4, 4, 2, TOK, HD), bf16),
            pltpu.VMEM((TOK, 2 * HD), f32),
            pltpu.VMEM((8, TOK, HD), f32),
            pltpu.VMEM((8, TOK, HD), bf16),
            pltpu.VMEM((8, TOK, HD), bf16),
            pltpu.VMEM((HD, 2 * TOK), bf16),
            pltpu.VMEM((2 * TOK, 2 * HD), bf16),
            pltpu.VMEM((8, TOK, HD), bf16),
            pltpu.VMEM((8, TOK, HD), bf16),
            pltpu.VMEM((65, PAGE, 2 * HD), f32),
            pltpu.VMEM((4, 4, 4, 16, 2 * HD), bf16),
            pltpu.VMEM((4, 4, 4, 16, 2 * HD), bf16),
            pltpu.VMEM((16, 4, 16, 2 * HD), bf16),
            pltpu.VMEM((64, 16, 2 * HD), bf16),
            pltpu.VMEM((4, 256, HD), bf16),
            pltpu.VMEM((4, 256, HD), bf16),
            pltpu.VMEM((4, 64, HD), bf16),
            pltpu.VMEM((4, 64, HD), bf16),
            pltpu.VMEM((4, 64, HD), bf16),
            pltpu.VMEM((4, 64, HD), bf16),
            pltpu.VMEM((4, 256, HD), bf16),
            pltpu.VMEM((64, 16, 2 * HD), bf16),
            dma((10,)),
            dma((1,)),
            dma((10, 3)),
            dma((10,)),
            dma((10, 3)),
            dma((10, 3)),
            dma((1,)),
            dma((4,)),
            dma((1,)),
            dma((1,)),
            dma((4,)),
            dma((4,)),
            dma((3,)),
            dma((3,)),
            dma((3,)),
            dma((5,)),
            dma((5,)),
            dma((9,)),
        ],
        compiler_params=pltpu.CompilerParams(
            collective_id=0, has_side_effects=True, vmem_limit_bytes=56 * 1024 * 1024
        ),
        cost_estimate=pl.CostEstimate(
            flops=2 * TOK * 8192 * 1280, bytes_accessed=12 << 20, transcendentals=8 * TOK * 1024
        ),
    )(hidden, w_query, w_key, w_value, cosine, sine, page_src, source_of, flag)
    return attended, kv.reshape(1, ctx_count, 2, PAGE, 2 * HD)


def solution(mesh):
    placed = (P("ctx", None), P("ctx", "tp"), P("ctx", "tp"), P("ctx", "tp"), P(), P())
    return jax.shard_map(
        on_device,
        mesh=mesh,
        in_specs=placed,
        out_specs=(P("ctx", "tp"), P("ctx", None, None, None, "tp")),
        check_vma=False,
    )
```

```python
import functools
import math

import jax
import jax.numpy as jnp
import numpy as np
from jax import lax
from jax.experimental import pallas as pl
from jax.experimental.pallas import tpu as pltpu
from jax.sharding import PartitionSpec as P

HD = 128
PAGE = 8
TOK = 512
MESH = pl.DeviceIdType.MESH

rope_theta = 500000.0
neg_large = -1e30


def kernel(
    hidden, w_query, w_key, w_value, inverse, block_order, page_map,
    attended, kv_cache,
    wkv, wq, hid, hid_p, acc, q_own, part_s, part_r,
    cosine, sine, kt, vs, qs, att, pg, p1, p2, p3, p4, m0, r0, m1, r1, r2, r3, r4, kvo,
    to_owner, to_block,
    loc, hid_l, send, rec_a, rec_b, rec_c, hid_s, hid_r, core_s, core_r, par_s, par_r,
    page_s, page_r, page_l, anc_s, anc_r, out_s,
):
    c = lax.axis_index("ctx")
    x = c // 16
    y = (c // 4) % 4
    z = c % 4
    half, parity = z // 2, z % 2
    beside = z + 1 - 2 * parity
    tp = lax.axis_index("tp")
    core = tp % 2
    coords = {"x": x, "y": y, "z": z}
    my_block = block_order[c]
    root = jnp.where(my_block == 0, 1.0, 0.0).astype(jnp.float32)

    def peer(axis, i):
        if axis == "x":
            return {"ctx": i * 16 + y * 4 + z}
        if axis == "y":
            return {"ctx": x * 16 + i * 4 + z}
        return {"ctx": x * 16 + y * 4 + i}

    def remote(src, dst, s, r, axis, i):
        pltpu.make_async_remote_copy(
            src_ref=src, dst_ref=dst, send_sem=s, recv_sem=r,
            device_id=peer(axis, i), device_id_type=MESH,
        ).start()

    def wait(ref, sem):
        pltpu.make_async_copy(ref, ref, sem).wait()

    def mine(g):
        return wkv.at[g, x, y, z] if g < 2 else wq.at[g - 2, x, y, half]

    def own_copy(g):
        if g == 0:
            src = w_key
        elif g == 1:
            src = w_value
        else:
            src = w_query.at[:, pl.ds((g - 2) * HD, HD)]
        return pltpu.make_async_copy(src, mine(g), loc.at[g])

    for g in range(10):
        own_copy(g).start()

    def hid_load(k, carry):
        pltpu.make_async_copy(
            hidden.at[:, pl.ds(pl.multiple_of(k * HD, HD), HD)],
            hid.at[k // 16, (k // 4) % 4, (k // 2) % 2, k % 2],
            hid_l.at[0],
        ).start()
        return carry

    lax.fori_loop(0, 64, hid_load, 0)

    barrier = pltpu.get_barrier_semaphore()
    for axis in "xyz":
        for d in (1, 2, 3):
            pl.semaphore_signal(
                barrier, inc=1, device_id=peer(axis, (coords[axis] + d) % 4), device_id_type=MESH
            )
    pl.semaphore_signal(
        barrier, inc=1, device_id={"tp": tp + 1 - 2 * core}, device_id_type=MESH
    )
    pl.semaphore_wait(barrier, 10)

    def a_start(g):
        own_copy(g).wait()
        if g < 2:
            for d in (1, 3, 2):
                remote(mine(g), mine(g), send.at[g, 0], rec_a.at[g], "z", (z + d) % 4)
        else:
            remote(mine(g), mine(g), send.at[g, 0], rec_a.at[g], "z", (z + 2) % 4)

    def a_done(g, sem):
        wait(wkv.at[g, x, y, 0:3] if g < 2 else wq.at[g - 2, x, y, 0], sem)

    def a_wait(g):
        a_done(g, rec_a.at[g])

    def layout(g, phase):
        w, k, n_half = (wkv, g, 2) if g < 2 else (wq, g - 2, 1)
        if g % 2 == 0:
            if phase == 1:
                return (
                    "y",
                    lambda i, h: w.at[k, x, i, pl.ds(n_half * h, n_half)],
                    lambda n: w.at[k, x, 0:n],
                )
            return "x", lambda i, h: w.at[k, i, pl.ds(2 * h, 2)], lambda n: w.at[k, 0:n]
        if phase == 1:
            return (
                "x",
                lambda i, h: w.at[k, i, y, pl.ds(n_half * h, n_half)],
                lambda n: w.at[k, 0:n, y],
            )
        return "y", lambda i, h: w.at[k, pl.ds(2 * h, 2), i], lambda n: w.at[k, :, 0:n]

    def rec(g, phase):
        return rec_b.at[g] if phase == 1 else rec_c.at[g]

    def ring_start(g, phase):
        axis, slab, _ = layout(g, phase)
        i = coords[axis]
        right, left = (i + 1) % 4, (i + 3) % 4
        s, r = send.at[g, phase], rec(g, phase)
        remote(slab(i, 0), slab(i, 0), s, r.at[0], axis, right)
        remote(slab(i, 1), slab(i, 1), s, r.at[1], axis, left)
        remote(slab(i, 1), slab(i, 1), s, r.at[2], axis, right)
        remote(slab(i, 0), slab(i, 0), s, r.at[2], axis, left)

    def ring_pass(g, phase):
        axis, slab, _ = layout(g, phase)
        i = coords[axis]
        right, left = (i + 1) % 4, (i + 3) % 4
        s, r = send.at[g, phase], rec(g, phase)
        wait(slab(left, 0), r.at[0])
        remote(slab(left, 0), slab(left, 0), s, r.at[2], axis, right)
        wait(slab(right, 1), r.at[1])
        remote(slab(right, 1), slab(right, 1), s, r.at[2], axis, left)

    def ring_wait(g, phase):
        wait(layout(g, phase)[2](2), rec(g, phase).at[2])

    b_start, b_pass, b_wait = (functools.partial(f, phase=1) for f in (ring_start, ring_pass, ring_wait))
    c_start, c_pass, c_wait = (functools.partial(f, phase=2) for f in (ring_start, ring_pass, ring_wait))

    def hid_piece(ref, k):
        return ref.at[k // 2, pl.ds(2 * (k % 2), 2)]

    def hid_start(j):
        k = core * 4 + j
        remote(
            hid.at[k // 2, pl.ds(2 * (k % 2), 2), :, 1 - parity], hid_piece(hid_p, k),
            hid_s.at[0], hid_r.at[j], "z", beside,
        )

    def hid_pass(j):
        k = core * 4 + j
        piece = hid_piece(hid_p, k)
        wait(piece, hid_r.at[j])
        pltpu.make_async_remote_copy(
            src_ref=piece, dst_ref=piece, send_sem=core_s.at[0], recv_sem=core_r.at[0],
            device_id={"tp": tp + 1 - 2 * core}, device_id_type=MESH,
        ).start()

    def project(left_of, k, w, pieces):
        rows = pieces * HD
        total = None
        for i in range(4):
            right = jnp.concatenate(
                [w[k, i].reshape(rows, HD), w[k + 1, i].reshape(rows, HD)], axis=1
            )
            d = jnp.dot(left_of(i), right, preferred_element_type=jnp.float32)
            total = d if total is None else total + d
        acc[...] = total

    def all_hidden(i):
        return jnp.concatenate(
            [hid[i, b, e, f] for b in range(4) for e in range(2) for f in range(2)], axis=1
        )

    def own_hidden(i):
        return jnp.concatenate(
            [hid[i, b, e, parity] for b in range(4) for e in range(2)], axis=1
        )

    def other_hidden(i):
        return jnp.concatenate([hid_p[i, b, e] for b in range(4) for e in range(2)], axis=1)

    def rotated(v):
        return v * cosine[...] + pltpu.roll(v, HD // 2, 1) * sine[...]

    def parts_other(g):
        h = g - 2
        project(other_hidden, h, wq, 8)
        part_s[h] = acc[:, :HD].astype(jnp.bfloat16)
        part_s[h + 1] = acc[:, HD:].astype(jnp.bfloat16)
        pair = pl.ds(h, 2)
        remote(part_s.at[pair], part_r.at[pair], par_s.at[h // 2], par_r.at[h // 2], "z", beside)

    def parts_own(g):
        h = g - 2
        project(own_hidden, h, wq, 8)
        q_own[h] = acc[:, :HD]
        q_own[h + 1] = acc[:, HD:]

    def part_wait(h, sem):
        wait(part_r.at[pl.ds(h, 2)], sem.at[h // 2])

    def queries(g):
        part_wait(g - 2, par_r)
        for h in (g - 2, g - 1):
            qs[h] = rotated(q_own[h] + part_r[h].astype(jnp.float32)).astype(jnp.bfloat16)

    factor = math.log2(math.e) / math.sqrt(HD)

    def anchor_ready():
        kt[:, 0:TOK] = r4[0:2].reshape(TOK, HD).astype(jnp.float32).T.astype(jnp.bfloat16)
        vs[0:TOK, 0:HD] = r4[2:4].reshape(TOK, HD)
        vs[:, HD:] = jnp.ones((2 * TOK, HD), jnp.bfloat16)

    def attend(g0):
        far_bias = root * neg_large

        def one(k, carry):
            h = g0 - 2 + k
            for b in range(2):
                n = 768 + 256 * b
                q = qs[h, b * 256:b * 256 + 256, :]
                scores = jnp.dot(q, kt[:, 0:n], preferred_element_type=jnp.float32)
                rows = lax.broadcasted_iota(jnp.int32, (256, 256), 0)
                columns = lax.broadcasted_iota(jnp.int32, (256, 256), 1)
                last = jnp.where(rows >= columns, scores[:, n - 256:], neg_large)
                far = scores[:, 0:TOK] + far_bias
                pieces = [far, last] if b == 0 else [far, scores[:, TOK:n - 256], last]
                top = functools.reduce(
                    jnp.maximum, [jnp.max(v, -1, keepdims=True) for v in pieces]
                )
                weights = jnp.concatenate(
                    [jnp.exp2((v - top) * factor).astype(jnp.bfloat16) for v in pieces], axis=1
                )
                result = jnp.dot(weights, vs[0:n, :], preferred_element_type=jnp.float32)
                att[h, b * 256:b * 256 + 256, :] = (
                    result[:, 0:HD] / result[:, HD:]
                ).astype(jnp.bfloat16)
            return carry

        one(0, 0)
        one(1, 0)
        for h in (g0 - 2, g0 - 1):
            out_copy(h).start()

    def out_copy(h):
        return pltpu.make_async_copy(att.at[h], attended.at[:, pl.ds(h * HD, HD)], out_s.at[h])

    def page_own(step):
        if step == 0:
            return pltpu.make_async_copy(p1.at[x], p2.at[x], page_l.at[0])
        if step == 1:
            return pltpu.make_async_copy(p2.at[:, y], p3.at[pl.ds(y * 4, 4)], page_l.at[1])
        return pltpu.make_async_copy(p3.at[:, z], p4.at[pl.ds(z * 16, 16)], page_l.at[2])

    def page_start(step):
        axis = "xyz"[step]
        page_own(step).start()
        for d in (1, 3, 2):
            i = (coords[axis] + d) % 4
            if step == 0:
                src, dst = p1.at[i], p2.at[x]
            elif step == 1:
                src, dst = p2.at[:, i], p3.at[pl.ds(y * 4, 4)]
            else:
                src, dst = p3.at[:, i], p4.at[pl.ds(z * 16, 16)]
            remote(src, dst, page_s.at[step], page_r.at[step], axis, i)

    def page_wait(step, sem):
        wait((p2.at[0:3], p3.at[0:12], p4.at[0:48])[step], sem.at[step])

    def page_take(step):
        page_own(step).wait()
        page_wait(step, page_r)

    anchor_steps = (
        ("x", m0, r0), ("y", m1, r1), ("z", None, r2), ("y", None, r3), ("x", None, r4),
    )

    def anchor_start(step):
        axis, parts, to = anchor_steps[step]
        i = coords[axis]
        if step == 0:
            r0[x] = m0[x]
        elif step == 1:
            total = r0[0] + r0[1] + r0[2] + r0[3]
            m1[...] = total.reshape(4, 64, HD)
            r1[y] = m1[y]
        elif step == 2:
            r2[z] = r1[0] + r1[1] + r1[2] + r1[3]
        elif step == 3:
            r3[y] = r2[0] + r2[1] + r2[2] + r2[3]
        else:
            r4[x] = r3[...].reshape(256, HD)
        for d in (1, 3, 2):
            j = (i + d) % 4
            src = parts.at[j] if parts is not None else to.at[i]
            remote(src, to.at[i], anc_s.at[step], anc_r.at[step], axis, j)

    def anchor_wait(step, sem):
        wait(anchor_steps[step][2].at[0:3], sem.at[step])

    def anchor_take(step):
        anchor_wait(step, anc_r)

    def keys_values():
        project(all_hidden, 0, wkv, 16)
        key = rotated(acc[:, :HD]).astype(jnp.bfloat16)
        value = acc[:, HD:].astype(jnp.bfloat16)
        wide_key, wide_value = key.astype(jnp.float32), value.astype(jnp.float32)
        kt[:, TOK:] = wide_key.T.astype(jnp.bfloat16)
        vs[TOK:, 0:HD] = value
        m0[0:2] = (wide_key * root).astype(jnp.bfloat16).reshape(2, 256, HD)
        m0[2:4] = (wide_value * root).astype(jnp.bfloat16).reshape(2, 256, HD)
        pg[:, 0:HD] = key
        pg[:, HD:] = value

    def angles():
        row = lax.broadcasted_iota(jnp.int32, (TOK, HD), 0)
        angle = (my_block * TOK + row).astype(jnp.float32) * inverse[...]
        lane = lax.broadcasted_iota(jnp.int32, (TOK, HD), 1)
        cosine[...] = jnp.cos(angle)
        turned = jnp.sin(angle)
        sine[...] = jnp.where(lane < HD // 2, -turned, turned)

    def spread_lanes(count, width, value_of):
        lane = lax.broadcasted_iota(jnp.int32, (1, count * width), 1)

        def one(k, row):
            return jnp.where(lane // width == k, value_of(k), row)

        return lane, lax.fori_loop(0, count, one, jnp.zeros_like(lane))

    def one_hot(rows, target):
        row = lax.broadcasted_iota(jnp.int32, (rows, target.shape[1]), 0)
        return jnp.where(row == target, 1.0, 0.0).astype(jnp.bfloat16)

    def page_targets():
        def owner(j):
            return page_map[my_block * 64 + j]

        lane, owners = spread_lanes(64, PAGE, owner)

        def rank(j, total):
            later = (owners == owner(j)) & (lane // PAGE > j)
            return total + jnp.where(later, 1, 0)

        ranks = lax.fori_loop(0, 64, rank, jnp.zeros_like(owners))
        to_owner[...] = (owners * 2 + ranks) * PAGE + lane % PAGE
        lane, blocks = spread_lanes(
            64, 16, lambda a: block_order[(a % 4) * 16 + (a // 4) % 4 * 4 + a // 16]
        )
        to_block[...] = blocks * 16 + lane % 16

    def deal_pages():
        dealt = jnp.dot(
            one_hot(1024, to_owner[...]), pg[...], preferred_element_type=jnp.float32
        )
        p1[...] = dealt.astype(jnp.bfloat16).reshape(4, 4, 4, 16, 2 * HD)

    def place_pages():
        placed = jnp.dot(
            one_hot(1024, to_block[...]), p4[...].reshape(1024, 2 * HD),
            preferred_element_type=jnp.float32,
        )
        kvo[...] = placed.astype(jnp.bfloat16).reshape(64, 16, 2 * HD)

    kv_copy = pltpu.make_async_copy(kvo, kv_cache, out_s.at[8])

    def each(f, *groups):
        for g in groups:
            f(g)

    each(a_start, 0, 1)
    for g in (0, 1):
        a_wait(g)
        b_start(g)
    each(a_start, *range(2, 10))
    wait(hid, hid_l.at[0])
    each(hid_start, 0, 1, 2, 3)
    each(b_pass, 0, 1)
    for g in (0, 1):
        b_wait(g)
        c_start(g)
    for g in (2, 3):
        a_wait(g)
        b_start(g)
    page_targets()
    angles()
    each(c_pass, 0, 1)
    for g in (4, 5):
        a_wait(g)
        b_start(g)
    each(b_pass, 2, 3)
    for g in (2, 3):
        b_wait(g)
        c_start(g)
    each(b_pass, 4, 5)
    hid_pass(0)
    each(c_wait, 0, 1)
    keys_values()
    anchor_start(0)
    each(c_pass, 2, 3)
    for g in (6, 7):
        a_wait(g)
        b_start(g)
    deal_pages()
    page_start(0)
    for g in (4, 5):
        b_wait(g)
        c_start(g)
    hid_pass(1)
    each(b_pass, 6, 7)
    anchor_take(0)
    anchor_start(1)
    each(c_wait, 2, 3)
    parts_own(2)
    each(c_pass, 4, 5)
    for g in (8, 9):
        a_wait(g)
        b_start(g)
    hid_pass(2)
    page_take(0)
    page_start(1)
    anchor_take(1)
    anchor_start(2)
    for g in (6, 7):
        b_wait(g)
        c_start(g)
    each(b_pass, 8, 9)
    anchor_take(2)
    anchor_start(3)
    hid_pass(3)
    each(c_wait, 4, 5)
    each(c_pass, 6, 7)
    parts_own(4)
    for g in (8, 9):
        b_wait(g)
        c_start(g)
    anchor_take(3)
    anchor_start(4)
    wait(hid_p.at[0:2], core_r.at[0])
    parts_other(2)
    parts_other(4)
    page_take(1)
    page_start(2)
    each(c_wait, 6, 7)
    parts_other(6)
    each(c_pass, 8, 9)
    parts_own(6)
    anchor_take(4)
    anchor_ready()
    queries(2)
    attend(2)
    queries(4)
    attend(4)
    each(c_wait, 8, 9)
    parts_other(8)
    parts_own(8)
    queries(6)
    attend(6)
    page_take(2)
    place_pages()
    kv_copy.start()
    queries(8)
    attend(8)

    for g in range(10):
        a_done(g, send.at[g, 0])
        wait(layout(g, 1)[2](3), send.at[g, 1])
        wait(layout(g, 2)[2](3), send.at[g, 2])
    wait(hid_p.at[0:2], hid_s.at[0])
    wait(hid_p.at[0:2], core_s.at[0])
    for h in (0, 2, 4, 6):
        part_wait(h, par_s)
    for step in range(3):
        page_wait(step, page_s)
    for step in range(5):
        anchor_wait(step, anc_s)
    for h in range(8):
        out_copy(h).wait()
    kv_copy.wait()


def on_device(hidden, w_query, w_key, w_value, block_order, page_map):
    ctx_count = lax.axis_size("ctx")
    exponent = np.arange(HD, dtype=np.float64) % (HD // 2) * (2.0 / HD)
    inverse = jnp.asarray((rope_theta ** -exponent).astype(np.float32)[None, :])

    hbm = pl.BlockSpec(memory_space=pl.ANY)
    vmem = pl.BlockSpec(memory_space=pltpu.VMEM)
    smem = pl.BlockSpec(memory_space=pltpu.SMEM)
    bf16, f32, dma = jnp.bfloat16, jnp.float32, pltpu.SemaphoreType.DMA
    attended, kv = pl.pallas_call(
        kernel,
        out_shape=(
            jax.ShapeDtypeStruct((TOK, 8 * HD), bf16),
            jax.ShapeDtypeStruct((64, 16, 2 * HD), bf16),
        ),
        in_specs=[hbm] * 4 + [vmem] + [smem] * 2,
        out_specs=(hbm, hbm),
        scratch_shapes=[
            pltpu.VMEM((2, 4, 4, 4, HD, HD), bf16),
            pltpu.VMEM((8, 4, 4, 2, HD, HD), bf16),
            pltpu.VMEM((4, 4, 2, 2, TOK, HD), bf16),
            pltpu.VMEM((4, 4, 2, TOK, HD), bf16),
            pltpu.VMEM((TOK, 2 * HD), f32),
            pltpu.VMEM((8, TOK, HD), f32),
            pltpu.VMEM((8, TOK, HD), bf16),
            pltpu.VMEM((8, TOK, HD), bf16),
            pltpu.VMEM((TOK, HD), f32),
            pltpu.VMEM((TOK, HD), f32),
            pltpu.VMEM((HD, 2 * TOK), bf16),
            pltpu.VMEM((2 * TOK, 2 * HD), bf16),
            pltpu.VMEM((8, TOK, HD), bf16),
            pltpu.VMEM((8, TOK, HD), bf16),
            pltpu.VMEM((TOK, 2 * HD), bf16),
            pltpu.VMEM((4, 4, 4, 16, 2 * HD), bf16),
            pltpu.VMEM((4, 4, 4, 16, 2 * HD), bf16),
            pltpu.VMEM((16, 4, 16, 2 * HD), bf16),
            pltpu.VMEM((64, 16, 2 * HD), bf16),
            pltpu.VMEM((4, 256, HD), bf16),
            pltpu.VMEM((4, 256, HD), bf16),
            pltpu.VMEM((4, 64, HD), bf16),
            pltpu.VMEM((4, 64, HD), bf16),
            pltpu.VMEM((4, 64, HD), bf16),
            pltpu.VMEM((4, 64, HD), bf16),
            pltpu.VMEM((4, 256, HD), bf16),
            pltpu.VMEM((64, 16, 2 * HD), bf16),
            pltpu.VMEM((1, TOK), jnp.int32),
            pltpu.VMEM((1, 1024), jnp.int32),
            dma((10,)),
            dma((1,)),
            dma((10, 3)),
            dma((10,)),
            dma((10, 3)),
            dma((10, 3)),
            dma((1,)),
            dma((4,)),
            dma((1,)),
            dma((1,)),
            dma((4,)),
            dma((4,)),
            dma((3,)),
            dma((3,)),
            dma((3,)),
            dma((5,)),
            dma((5,)),
            dma((9,)),
        ],
        compiler_params=pltpu.CompilerParams(
            collective_id=0, has_side_effects=True, vmem_limit_bytes=56 * 1024 * 1024
        ),
        cost_estimate=pl.CostEstimate(
            flops=2 * TOK * 8192 * 1280, bytes_accessed=12 << 20, transcendentals=8 * TOK * 1024
        ),
    )(hidden, w_query, w_key, w_value, inverse, block_order, page_map[:, 0])
    return attended, kv.reshape(1, ctx_count, 2, PAGE, 2 * HD)


def solution(mesh):
    placed = (P("ctx", None), P("ctx", "tp"), P("ctx", "tp"), P("ctx", "tp"), P(), P())
    return jax.shard_map(
        on_device,
        mesh=mesh,
        in_specs=placed,
        out_specs=(P("ctx", "tp"), P("ctx", None, None, None, "tp")),
        check_vma=False,
    )
```

```python
import functools
import math

import jax
import jax.numpy as jnp
import numpy as np
from jax import lax
from jax.experimental import pallas as pl
from jax.experimental.pallas import tpu as pltpu
from jax.sharding import PartitionSpec as P

HD = 128
PAGE = 8
TOK = 512
MESH = pl.DeviceIdType.MESH

rope_theta = 500000.0
neg_large = -1e30


def kernel(
    hidden, w_query, w_key, w_value, inverse, block_order, page_map,
    attended, kv_cache,
    wkv, wq, hid, hid_p, acc, q_own, part_s, part_r,
    cosine, sine, kt, vs, qs, att, pg, p1, p2, p3, p4, m0, r0, m1, r1, r2, r3, r4, kvo,
    to_owner, to_block,
    loc, hid_l, send, rec_a, rec_b, rec_c, hid_s, hid_r, core_s, core_r, par_s, par_r,
    page_s, page_r, page_l, anc_s, anc_r, out_s,
):
    c = lax.axis_index("ctx")
    x = c // 16
    y = (c // 4) % 4
    z = c % 4
    half, parity = z // 2, z % 2
    beside = z + 1 - 2 * parity
    tp = lax.axis_index("tp")
    core = tp % 2
    coords = {"x": x, "y": y, "z": z}
    my_block = block_order[c]
    root = jnp.where(my_block == 0, 1.0, 0.0).astype(jnp.float32)

    def peer(axis, i):
        if axis == "x":
            return {"ctx": i * 16 + y * 4 + z}
        if axis == "y":
            return {"ctx": x * 16 + i * 4 + z}
        return {"ctx": x * 16 + y * 4 + i}

    def remote(src, dst, s, r, axis, i):
        pltpu.make_async_remote_copy(
            src_ref=src, dst_ref=dst, send_sem=s, recv_sem=r,
            device_id=peer(axis, i), device_id_type=MESH,
        ).start()

    def wait(ref, sem):
        pltpu.make_async_copy(ref, ref, sem).wait()

    def mine(g):
        return wkv.at[g, x, y, z] if g < 2 else wq.at[g - 2, x, y, half]

    def own_copy(g):
        if g == 0:
            src = w_key
        elif g == 1:
            src = w_value
        else:
            src = w_query.at[:, pl.ds((g - 2) * HD, HD)]
        return pltpu.make_async_copy(src, mine(g), loc.at[g])

    for g in range(10):
        own_copy(g).start()

    def hid_load(k, carry):
        pltpu.make_async_copy(
            hidden.at[:, pl.ds(pl.multiple_of(k * HD, HD), HD)],
            hid.at[k // 16, (k // 4) % 4, (k // 2) % 2, k % 2],
            hid_l.at[0],
        ).start()
        return carry

    lax.fori_loop(0, 64, hid_load, 0)

    barrier = pltpu.get_barrier_semaphore()
    for axis in "xyz":
        for d in (1, 2, 3):
            pl.semaphore_signal(
                barrier, inc=1, device_id=peer(axis, (coords[axis] + d) % 4), device_id_type=MESH
            )
    pl.semaphore_signal(
        barrier, inc=1, device_id={"tp": tp + 1 - 2 * core}, device_id_type=MESH
    )
    pl.semaphore_wait(barrier, 10)

    def a_start(g):
        own_copy(g).wait()
        if g < 2:
            for d in (1, 3, 2):
                remote(mine(g), mine(g), send.at[g, 0], rec_a.at[g], "z", (z + d) % 4)
        else:
            remote(mine(g), mine(g), send.at[g, 0], rec_a.at[g], "z", (z + 2) % 4)

    def a_done(g, sem):
        wait(wkv.at[g, x, y, 0:3] if g < 2 else wq.at[g - 2, x, y, 0], sem)

    def a_wait(g):
        a_done(g, rec_a.at[g])

    def layout(g, phase):
        w, k, n_half = (wkv, g, 2) if g < 2 else (wq, g - 2, 1)
        if g % 2 == 0:
            if phase == 1:
                return (
                    "y",
                    lambda i, h: w.at[k, x, i, pl.ds(n_half * h, n_half)],
                    lambda n: w.at[k, x, 0:n],
                )
            return "x", lambda i, h: w.at[k, i, pl.ds(2 * h, 2)], lambda n: w.at[k, 0:n]
        if phase == 1:
            return (
                "x",
                lambda i, h: w.at[k, i, y, pl.ds(n_half * h, n_half)],
                lambda n: w.at[k, 0:n, y],
            )
        return "y", lambda i, h: w.at[k, pl.ds(2 * h, 2), i], lambda n: w.at[k, :, 0:n]

    def rec(g, phase):
        return rec_b.at[g] if phase == 1 else rec_c.at[g]

    def ring_start(g, phase):
        axis, slab, _ = layout(g, phase)
        i = coords[axis]
        right, left = (i + 1) % 4, (i + 3) % 4
        s, r = send.at[g, phase], rec(g, phase)
        remote(slab(i, 0), slab(i, 0), s, r.at[0], axis, right)
        remote(slab(i, 1), slab(i, 1), s, r.at[1], axis, left)
        remote(slab(i, 1), slab(i, 1), s, r.at[2], axis, right)
        remote(slab(i, 0), slab(i, 0), s, r.at[2], axis, left)

    def ring_pass(g, phase):
        axis, slab, _ = layout(g, phase)
        i = coords[axis]
        right, left = (i + 1) % 4, (i + 3) % 4
        s, r = send.at[g, phase], rec(g, phase)
        wait(slab(left, 0), r.at[0])
        remote(slab(left, 0), slab(left, 0), s, r.at[2], axis, right)
        wait(slab(right, 1), r.at[1])
        remote(slab(right, 1), slab(right, 1), s, r.at[2], axis, left)

    def ring_wait(g, phase):
        wait(layout(g, phase)[2](2), rec(g, phase).at[2])

    b_start, b_pass, b_wait = (functools.partial(f, phase=1) for f in (ring_start, ring_pass, ring_wait))
    c_start, c_pass, c_wait = (functools.partial(f, phase=2) for f in (ring_start, ring_pass, ring_wait))

    def hid_piece(ref, k):
        return ref.at[k // 2, pl.ds(2 * (k % 2), 2)]

    def hid_start(j):
        k = core * 4 + j
        remote(
            hid.at[k // 2, pl.ds(2 * (k % 2), 2), :, 1 - parity], hid_piece(hid_p, k),
            hid_s.at[0], hid_r.at[j], "z", beside,
        )

    def hid_pass(j):
        k = core * 4 + j
        piece = hid_piece(hid_p, k)
        wait(piece, hid_r.at[j])
        pltpu.make_async_remote_copy(
            src_ref=piece, dst_ref=piece, send_sem=core_s.at[0], recv_sem=core_r.at[0],
            device_id={"tp": tp + 1 - 2 * core}, device_id_type=MESH,
        ).start()

    def project(left_of, k, w, pieces):
        rows = pieces * HD
        total = None
        for i in range(4):
            right = jnp.concatenate(
                [w[k, i].reshape(rows, HD), w[k + 1, i].reshape(rows, HD)], axis=1
            )
            d = jnp.dot(left_of(i), right, preferred_element_type=jnp.float32)
            total = d if total is None else total + d
        acc[...] = total

    def all_hidden(i):
        return jnp.concatenate(
            [hid[i, b, e, f] for b in range(4) for e in range(2) for f in range(2)], axis=1
        )

    def own_hidden(i):
        return jnp.concatenate(
            [hid[i, b, e, parity] for b in range(4) for e in range(2)], axis=1
        )

    def other_hidden(i):
        return jnp.concatenate([hid_p[i, b, e] for b in range(4) for e in range(2)], axis=1)

    def rotated(v):
        return v * cosine[...] + pltpu.roll(v, HD // 2, 1) * sine[...]

    def parts_other(g):
        h = g - 2
        project(other_hidden, h, wq, 8)
        part_s[h] = acc[:, :HD].astype(jnp.bfloat16)
        part_s[h + 1] = acc[:, HD:].astype(jnp.bfloat16)
        pair = pl.ds(h, 2)
        remote(part_s.at[pair], part_r.at[pair], par_s.at[h // 2], par_r.at[h // 2], "z", beside)

    def parts_own(g):
        h = g - 2
        project(own_hidden, h, wq, 8)
        q_own[h] = acc[:, :HD]
        q_own[h + 1] = acc[:, HD:]

    def part_wait(h, sem):
        wait(part_r.at[pl.ds(h, 2)], sem.at[h // 2])

    def queries(g):
        part_wait(g - 2, par_r)
        for h in (g - 2, g - 1):
            qs[h] = rotated(q_own[h] + part_r[h].astype(jnp.float32)).astype(jnp.bfloat16)

    factor = math.log2(math.e) / math.sqrt(HD)

    def anchor_ready():
        kt[:, 0:TOK] = r4[0:2].reshape(TOK, HD).astype(jnp.float32).T.astype(jnp.bfloat16)
        vs[0:TOK, 0:HD] = r4[2:4].reshape(TOK, HD)
        vs[:, HD:] = jnp.ones((2 * TOK, HD), jnp.bfloat16)

    def attend(g0):
        far_bias = root * neg_large

        def one(k, carry):
            h = g0 - 2 + k
            for b in range(2):
                n = 768 + 256 * b
                q = qs[h, b * 256:b * 256 + 256, :]
                scores = jnp.dot(q, kt[:, 0:n], preferred_element_type=jnp.float32)
                rows = lax.broadcasted_iota(jnp.int32, (256, 256), 0)
                columns = lax.broadcasted_iota(jnp.int32, (256, 256), 1)
                last = jnp.where(rows >= columns, scores[:, n - 256:], neg_large)
                far = scores[:, 0:TOK] + far_bias
                pieces = [far, last] if b == 0 else [far, scores[:, TOK:n - 256], last]
                top = functools.reduce(
                    jnp.maximum, [jnp.max(v, -1, keepdims=True) for v in pieces]
                )
                weights = jnp.concatenate(
                    [jnp.exp2((v - top) * factor).astype(jnp.bfloat16) for v in pieces], axis=1
                )
                result = jnp.dot(weights, vs[0:n, :], preferred_element_type=jnp.float32)
                att[h, b * 256:b * 256 + 256, :] = (
                    result[:, 0:HD] / result[:, HD:]
                ).astype(jnp.bfloat16)
            return carry

        one(0, 0)
        one(1, 0)
        for h in (g0 - 2, g0 - 1):
            out_copy(h).start()

    def out_copy(h):
        return pltpu.make_async_copy(att.at[h], attended.at[:, pl.ds(h * HD, HD)], out_s.at[h])

    def page_own(step):
        if step == 0:
            return pltpu.make_async_copy(p1.at[x], p2.at[x], page_l.at[0])
        if step == 1:
            return pltpu.make_async_copy(p2.at[:, y], p3.at[pl.ds(y * 4, 4)], page_l.at[1])
        return pltpu.make_async_copy(p3.at[:, z], p4.at[pl.ds(z * 16, 16)], page_l.at[2])

    def page_start(step):
        axis = "xyz"[step]
        page_own(step).start()
        for d in (1, 3, 2):
            i = (coords[axis] + d) % 4
            if step == 0:
                src, dst = p1.at[i], p2.at[x]
            elif step == 1:
                src, dst = p2.at[:, i], p3.at[pl.ds(y * 4, 4)]
            else:
                src, dst = p3.at[:, i], p4.at[pl.ds(z * 16, 16)]
            remote(src, dst, page_s.at[step], page_r.at[step], axis, i)

    def page_wait(step, sem):
        wait((p2.at[0:3], p3.at[0:12], p4.at[0:48])[step], sem.at[step])

    def page_take(step):
        page_own(step).wait()
        page_wait(step, page_r)

    anchor_steps = (
        ("x", m0, r0), ("y", m1, r1), ("z", None, r2), ("y", None, r3), ("x", None, r4),
    )

    def anchor_start(step):
        axis, parts, to = anchor_steps[step]
        i = coords[axis]
        if step == 0:
            r0[x] = m0[x]
        elif step == 1:
            total = r0[0] + r0[1] + r0[2] + r0[3]
            m1[...] = total.reshape(4, 64, HD)
            r1[y] = m1[y]
        elif step == 2:
            r2[z] = r1[0] + r1[1] + r1[2] + r1[3]
        elif step == 3:
            r3[y] = r2[0] + r2[1] + r2[2] + r2[3]
        else:
            r4[x] = r3[...].reshape(256, HD)
        for d in (1, 3, 2):
            j = (i + d) % 4
            src = parts.at[j] if parts is not None else to.at[i]
            remote(src, to.at[i], anc_s.at[step], anc_r.at[step], axis, j)

    def anchor_wait(step, sem):
        wait(anchor_steps[step][2].at[0:3], sem.at[step])

    def anchor_take(step):
        anchor_wait(step, anc_r)

    def keys_values():
        project(all_hidden, 0, wkv, 16)
        key = rotated(acc[:, :HD]).astype(jnp.bfloat16)
        value = acc[:, HD:].astype(jnp.bfloat16)
        wide_key, wide_value = key.astype(jnp.float32), value.astype(jnp.float32)
        kt[:, TOK:] = wide_key.T.astype(jnp.bfloat16)
        vs[TOK:, 0:HD] = value
        m0[0:2] = (wide_key * root).astype(jnp.bfloat16).reshape(2, 256, HD)
        m0[2:4] = (wide_value * root).astype(jnp.bfloat16).reshape(2, 256, HD)
        pg[:, 0:HD] = key
        pg[:, HD:] = value

    def angles():
        row = lax.broadcasted_iota(jnp.int32, (TOK, HD), 0)
        angle = (my_block * TOK + row).astype(jnp.float32) * inverse[...]
        lane = lax.broadcasted_iota(jnp.int32, (TOK, HD), 1)
        cosine[...] = jnp.cos(angle)
        turned = jnp.sin(angle)
        sine[...] = jnp.where(lane < HD // 2, -turned, turned)

    def spread_lanes(count, width, value_of):
        lane = lax.broadcasted_iota(jnp.int32, (1, count * width), 1)

        def one(k, row):
            return jnp.where(lane // width == k, value_of(k), row)

        return lane, lax.fori_loop(0, count, one, jnp.zeros_like(lane))

    def one_hot(rows, target):
        row = lax.broadcasted_iota(jnp.int32, (rows, target.shape[1]), 0)
        return jnp.where(row == target, 1.0, 0.0).astype(jnp.bfloat16)

    def page_targets():
        def owner(j):
            return page_map[my_block * 64 + j]

        lane, owners = spread_lanes(64, PAGE, owner)

        def rank(j, total):
            later = (owners == owner(j)) & (lane // PAGE > j)
            return total + jnp.where(later, 1, 0)

        ranks = lax.fori_loop(0, 64, rank, jnp.zeros_like(owners))
        to_owner[...] = (owners * 2 + ranks) * PAGE + lane % PAGE
        lane, blocks = spread_lanes(
            64, 16, lambda a: block_order[(a % 4) * 16 + (a // 4) % 4 * 4 + a // 16]
        )
        to_block[...] = blocks * 16 + lane % 16

    def deal_pages():
        dealt = jnp.dot(
            one_hot(1024, to_owner[...]), pg[...], preferred_element_type=jnp.float32
        )
        p1[...] = dealt.astype(jnp.bfloat16).reshape(4, 4, 4, 16, 2 * HD)

    def place_pages():
        placed = jnp.dot(
            one_hot(1024, to_block[...]), p4[...].reshape(1024, 2 * HD),
            preferred_element_type=jnp.float32,
        )
        kvo[...] = placed.astype(jnp.bfloat16).reshape(64, 16, 2 * HD)

    kv_copy = pltpu.make_async_copy(kvo, kv_cache, out_s.at[8])

    def each(f, *groups):
        for g in groups:
            f(g)

    each(a_start, 0, 1)
    for g in (0, 1):
        a_wait(g)
        b_start(g)
    each(a_start, *range(2, 10))
    wait(hid, hid_l.at[0])
    each(hid_start, 0, 1, 2, 3)
    each(b_pass, 0, 1)
    for g in (0, 1):
        b_wait(g)
        c_start(g)
    for g in (2, 3):
        a_wait(g)
        b_start(g)
    page_targets()
    angles()
    each(c_pass, 0, 1)
    for g in (4, 5):
        a_wait(g)
        b_start(g)
    each(b_pass, 2, 3)
    for g in (2, 3):
        b_wait(g)
        c_start(g)
    each(b_pass, 4, 5)
    hid_pass(0)
    each(c_wait, 0, 1)
    keys_values()
    anchor_start(0)
    each(c_pass, 2, 3)
    for g in (6, 7):
        a_wait(g)
        b_start(g)
    deal_pages()
    page_start(0)
    each(b_wait, 4, 5)
    hid_pass(1)
    each(c_start, 4, 5)
    each(b_pass, 6, 7)
    anchor_take(0)
    anchor_start(1)
    each(c_wait, 2, 3)
    hid_pass(2)
    parts_own(2)
    each(c_pass, 4, 5)
    for g in (8, 9):
        a_wait(g)
        b_start(g)
    page_take(0)
    page_start(1)
    anchor_take(1)
    anchor_start(2)
    each(b_wait, 6, 7)
    hid_pass(3)
    each(c_start, 6, 7)
    each(b_pass, 8, 9)
    anchor_take(2)
    anchor_start(3)
    page_take(1)
    page_start(2)
    each(c_wait, 4, 5)
    each(c_pass, 6, 7)
    wait(hid_p.at[0:2], core_r.at[0])
    parts_other(2)
    parts_other(4)
    for g in (8, 9):
        b_wait(g)
        c_start(g)
    anchor_take(3)
    anchor_start(4)
    parts_own(4)
    each(c_wait, 6, 7)
    parts_other(6)
    each(c_pass, 8, 9)
    parts_own(6)
    anchor_take(4)
    anchor_ready()
    queries(2)
    attend(2)
    queries(4)
    attend(4)
    each(c_wait, 8, 9)
    parts_other(8)
    parts_own(8)
    queries(6)
    attend(6)
    page_take(2)
    place_pages()
    kv_copy.start()
    queries(8)
    attend(8)

    for g in range(10):
        a_done(g, send.at[g, 0])
        wait(layout(g, 1)[2](3), send.at[g, 1])
        wait(layout(g, 2)[2](3), send.at[g, 2])
    wait(hid_p.at[0:2], hid_s.at[0])
    wait(hid_p.at[0:2], core_s.at[0])
    for h in (0, 2, 4, 6):
        part_wait(h, par_s)
    for step in range(3):
        page_wait(step, page_s)
    for step in range(5):
        anchor_wait(step, anc_s)
    for h in range(8):
        out_copy(h).wait()
    kv_copy.wait()


def on_device(hidden, w_query, w_key, w_value, block_order, page_map):
    ctx_count = lax.axis_size("ctx")
    exponent = np.arange(HD, dtype=np.float64) % (HD // 2) * (2.0 / HD)
    inverse = jnp.asarray((rope_theta ** -exponent).astype(np.float32)[None, :])

    hbm = pl.BlockSpec(memory_space=pl.ANY)
    vmem = pl.BlockSpec(memory_space=pltpu.VMEM)
    smem = pl.BlockSpec(memory_space=pltpu.SMEM)
    bf16, f32, dma = jnp.bfloat16, jnp.float32, pltpu.SemaphoreType.DMA
    attended, kv = pl.pallas_call(
        kernel,
        out_shape=(
            jax.ShapeDtypeStruct((TOK, 8 * HD), bf16),
            jax.ShapeDtypeStruct((64, 16, 2 * HD), bf16),
        ),
        in_specs=[hbm] * 4 + [vmem] + [smem] * 2,
        out_specs=(hbm, hbm),
        scratch_shapes=[
            pltpu.VMEM((2, 4, 4, 4, HD, HD), bf16),
            pltpu.VMEM((8, 4, 4, 2, HD, HD), bf16),
            pltpu.VMEM((4, 4, 2, 2, TOK, HD), bf16),
            pltpu.VMEM((4, 4, 2, TOK, HD), bf16),
            pltpu.VMEM((TOK, 2 * HD), f32),
            pltpu.VMEM((8, TOK, HD), f32),
            pltpu.VMEM((8, TOK, HD), bf16),
            pltpu.VMEM((8, TOK, HD), bf16),
            pltpu.VMEM((TOK, HD), f32),
            pltpu.VMEM((TOK, HD), f32),
            pltpu.VMEM((HD, 2 * TOK), bf16),
            pltpu.VMEM((2 * TOK, 2 * HD), bf16),
            pltpu.VMEM((8, TOK, HD), bf16),
            pltpu.VMEM((8, TOK, HD), bf16),
            pltpu.VMEM((TOK, 2 * HD), bf16),
            pltpu.VMEM((4, 4, 4, 16, 2 * HD), bf16),
            pltpu.VMEM((4, 4, 4, 16, 2 * HD), bf16),
            pltpu.VMEM((16, 4, 16, 2 * HD), bf16),
            pltpu.VMEM((64, 16, 2 * HD), bf16),
            pltpu.VMEM((4, 256, HD), bf16),
            pltpu.VMEM((4, 256, HD), bf16),
            pltpu.VMEM((4, 64, HD), bf16),
            pltpu.VMEM((4, 64, HD), bf16),
            pltpu.VMEM((4, 64, HD), bf16),
            pltpu.VMEM((4, 64, HD), bf16),
            pltpu.VMEM((4, 256, HD), bf16),
            pltpu.VMEM((64, 16, 2 * HD), bf16),
            pltpu.VMEM((1, TOK), jnp.int32),
            pltpu.VMEM((1, 1024), jnp.int32),
            dma((10,)),
            dma((1,)),
            dma((10, 3)),
            dma((10,)),
            dma((10, 3)),
            dma((10, 3)),
            dma((1,)),
            dma((4,)),
            dma((1,)),
            dma((1,)),
            dma((4,)),
            dma((4,)),
            dma((3,)),
            dma((3,)),
            dma((3,)),
            dma((5,)),
            dma((5,)),
            dma((9,)),
        ],
        compiler_params=pltpu.CompilerParams(
            collective_id=0, has_side_effects=True, vmem_limit_bytes=56 * 1024 * 1024
        ),
        cost_estimate=pl.CostEstimate(
            flops=2 * TOK * 8192 * 1280, bytes_accessed=12 << 20, transcendentals=8 * TOK * 1024
        ),
    )(hidden, w_query, w_key, w_value, inverse, block_order, page_map[:, 0])
    return attended, kv.reshape(1, ctx_count, 2, PAGE, 2 * HD)


def solution(mesh):
    placed = (P("ctx", None), P("ctx", "tp"), P("ctx", "tp"), P("ctx", "tp"), P(), P())
    return jax.shard_map(
        on_device,
        mesh=mesh,
        in_specs=placed,
        out_specs=(P("ctx", "tp"), P("ctx", None, None, None, "tp")),
        check_vma=False,
    )
```

```python
import functools
import math

import jax
import jax.numpy as jnp
import numpy as np
from jax import lax
from jax.experimental import pallas as pl
from jax.experimental.pallas import tpu as pltpu
from jax.sharding import PartitionSpec as P

HD = 128
PAGE = 8
TOK = 512
MESH = pl.DeviceIdType.MESH

rope_theta = 500000.0
neg_large = -1e30


def kernel(
    hidden, w_query, w_key, w_value, inverse, block_order, page_map,
    attended, kv_cache,
    wkv, wq, hid, hid_p, acc, q_own, part_s, part_r,
    cosine, sine, kt, vs, qs, att, pg, p1, p2, p3, p4, m0, r0, m1, r1, r2, r3, r4, kvo,
    to_owner, to_block,
    loc, hid_l, send, rec_a, rec_b, rec_c, hid_s, hid_r, core_s, core_r, par_s, par_r,
    page_s, page_r, page_l, anc_s, anc_r, out_s,
):
    c = lax.axis_index("ctx")
    x = c // 16
    y = (c // 4) % 4
    z = c % 4
    half, parity = z // 2, z % 2
    beside = z + 1 - 2 * parity
    tp = lax.axis_index("tp")
    core = tp % 2
    coords = {"x": x, "y": y, "z": z}
    my_block = block_order[c]
    root = jnp.where(my_block == 0, 1.0, 0.0).astype(jnp.float32)

    def peer(axis, i):
        if axis == "x":
            return {"ctx": i * 16 + y * 4 + z}
        if axis == "y":
            return {"ctx": x * 16 + i * 4 + z}
        return {"ctx": x * 16 + y * 4 + i}

    def remote(src, dst, s, r, axis, i):
        pltpu.make_async_remote_copy(
            src_ref=src, dst_ref=dst, send_sem=s, recv_sem=r,
            device_id=peer(axis, i), device_id_type=MESH,
        ).start()

    def wait(ref, sem):
        pltpu.make_async_copy(ref, ref, sem).wait()

    def mine(g):
        return wkv.at[g, x, y, z] if g < 2 else wq.at[g - 2, x, y, half]

    def own_copy(g):
        if g == 0:
            src = w_key
        elif g == 1:
            src = w_value
        else:
            src = w_query.at[:, pl.ds((g - 2) * HD, HD)]
        return pltpu.make_async_copy(src, mine(g), loc.at[g])

    for g in range(2):
        own_copy(g).start()

    def hid_load(k, carry):
        pltpu.make_async_copy(
            hidden.at[:, pl.ds(pl.multiple_of(k * HD, HD), HD)],
            hid.at[k // 16, (k // 4) % 4, (k // 2) % 2, k % 2],
            hid_l.at[0],
        ).start()
        return carry

    barrier = pltpu.get_barrier_semaphore()
    for axis in "xyz":
        for d in (1, 2, 3):
            pl.semaphore_signal(
                barrier, inc=1, device_id=peer(axis, (coords[axis] + d) % 4), device_id_type=MESH
            )
    pl.semaphore_signal(
        barrier, inc=1, device_id={"tp": tp + 1 - 2 * core}, device_id_type=MESH
    )
    pl.semaphore_wait(barrier, 10)

    def a_start(g):
        own_copy(g).wait()
        if g < 2:
            for d in (1, 3, 2):
                remote(mine(g), mine(g), send.at[g, 0], rec_a.at[g], "z", (z + d) % 4)
        else:
            remote(mine(g), mine(g), send.at[g, 0], rec_a.at[g], "z", (z + 2) % 4)

    def a_done(g, sem):
        wait(wkv.at[g, x, y, 0:3] if g < 2 else wq.at[g - 2, x, y, 0], sem)

    def a_wait(g):
        a_done(g, rec_a.at[g])

    def layout(g, phase):
        w, k, n_half = (wkv, g, 2) if g < 2 else (wq, g - 2, 1)
        if g % 2 == 0:
            if phase == 1:
                return (
                    "y",
                    lambda i, h: w.at[k, x, i, pl.ds(n_half * h, n_half)],
                    lambda n: w.at[k, x, 0:n],
                )
            return "x", lambda i, h: w.at[k, i, pl.ds(2 * h, 2)], lambda n: w.at[k, 0:n]
        if phase == 1:
            return (
                "x",
                lambda i, h: w.at[k, i, y, pl.ds(n_half * h, n_half)],
                lambda n: w.at[k, 0:n, y],
            )
        return "y", lambda i, h: w.at[k, pl.ds(2 * h, 2), i], lambda n: w.at[k, :, 0:n]

    def rec(g, phase):
        return rec_b.at[g] if phase == 1 else rec_c.at[g]

    def ring_start(g, phase):
        axis, slab, _ = layout(g, phase)
        i = coords[axis]
        right, left = (i + 1) % 4, (i + 3) % 4
        s, r = send.at[g, phase], rec(g, phase)
        remote(slab(i, 0), slab(i, 0), s, r.at[0], axis, right)
        remote(slab(i, 1), slab(i, 1), s, r.at[1], axis, left)
        remote(slab(i, 1), slab(i, 1), s, r.at[2], axis, right)
        remote(slab(i, 0), slab(i, 0), s, r.at[2], axis, left)

    def ring_pass(g, phase):
        axis, slab, _ = layout(g, phase)
        i = coords[axis]
        right, left = (i + 1) % 4, (i + 3) % 4
        s, r = send.at[g, phase], rec(g, phase)
        wait(slab(left, 0), r.at[0])
        remote(slab(left, 0), slab(left, 0), s, r.at[2], axis, right)
        wait(slab(right, 1), r.at[1])
        remote(slab(right, 1), slab(right, 1), s, r.at[2], axis, left)

    def ring_wait(g, phase):
        wait(layout(g, phase)[2](2), rec(g, phase).at[2])

    b_start, b_pass, b_wait = (functools.partial(f, phase=1) for f in (ring_start, ring_pass, ring_wait))
    c_start, c_pass, c_wait = (functools.partial(f, phase=2) for f in (ring_start, ring_pass, ring_wait))

    def hid_piece(ref, k):
        return ref.at[k // 2, pl.ds(2 * (k % 2), 2)]

    def hid_start(j):
        k = core * 4 + j
        remote(
            hid.at[k // 2, pl.ds(2 * (k % 2), 2), :, 1 - parity], hid_piece(hid_p, k),
            hid_s.at[0], hid_r.at[j], "z", beside,
        )

    def hid_pass(j):
        k = core * 4 + j
        piece = hid_piece(hid_p, k)
        wait(piece, hid_r.at[j])
        pltpu.make_async_remote_copy(
            src_ref=piece, dst_ref=piece, send_sem=core_s.at[0], recv_sem=core_r.at[0],
            device_id={"tp": tp + 1 - 2 * core}, device_id_type=MESH,
        ).start()

    def project(left_of, k, w, pieces):
        rows = pieces * HD
        total = None
        for i in range(4):
            right = jnp.concatenate(
                [w[k, i].reshape(rows, HD), w[k + 1, i].reshape(rows, HD)], axis=1
            )
            d = jnp.dot(left_of(i), right, preferred_element_type=jnp.float32)
            total = d if total is None else total + d
        acc[...] = total

    def all_hidden(i):
        return jnp.concatenate(
            [hid[i, b, e, f] for b in range(4) for e in range(2) for f in range(2)], axis=1
        )

    def own_hidden(i):
        return jnp.concatenate(
            [hid[i, b, e, parity] for b in range(4) for e in range(2)], axis=1
        )

    def other_hidden(i):
        return jnp.concatenate([hid_p[i, b, e] for b in range(4) for e in range(2)], axis=1)

    def rotated(v):
        return v * cosine[...] + pltpu.roll(v, HD // 2, 1) * sine[...]

    def parts_other(g):
        h = g - 2
        project(other_hidden, h, wq, 8)
        part_s[h] = acc[:, :HD].astype(jnp.bfloat16)
        part_s[h + 1] = acc[:, HD:].astype(jnp.bfloat16)
        for k in (h, h + 1):
            remote(part_s.at[k], part_r.at[k], par_s.at[k], par_r.at[k], "z", beside)

    def parts_own(g):
        h = g - 2
        project(own_hidden, h, wq, 8)
        q_own[h] = acc[:, :HD]
        q_own[h + 1] = acc[:, HD:]

    def part_wait(h, sem):
        wait(part_r.at[h], sem.at[h])

    def query(h):
        part_wait(h, par_r)
        qs[h] = rotated(q_own[h] + part_r[h].astype(jnp.float32)).astype(jnp.bfloat16)

    def queries(g):
        query(g - 2)
        query(g - 1)

    factor = math.log2(math.e) / math.sqrt(HD)

    def anchor_ready():
        kt[:, 0:TOK] = r4[0:2].reshape(TOK, HD).astype(jnp.float32).T.astype(jnp.bfloat16)
        vs[0:TOK, 0:HD] = r4[2:4].reshape(TOK, HD)
        vs[:, HD:] = jnp.ones((2 * TOK, HD), jnp.bfloat16)

    def attend(*heads):
        far_bias = root * neg_large

        def one(h):
            for b in range(2):
                n = 768 + 256 * b
                q = qs[h, b * 256:b * 256 + 256, :]
                scores = jnp.dot(q, kt[:, 0:n], preferred_element_type=jnp.float32)
                rows = lax.broadcasted_iota(jnp.int32, (256, 256), 0)
                columns = lax.broadcasted_iota(jnp.int32, (256, 256), 1)
                last = jnp.where(rows >= columns, scores[:, n - 256:], neg_large)
                far = scores[:, 0:TOK] + far_bias
                pieces = [far, last] if b == 0 else [far, scores[:, TOK:n - 256], last]
                top = functools.reduce(
                    jnp.maximum, [jnp.max(v, -1, keepdims=True) for v in pieces]
                )
                weights = jnp.concatenate(
                    [jnp.exp2((v - top) * factor).astype(jnp.bfloat16) for v in pieces], axis=1
                )
                result = jnp.dot(weights, vs[0:n, :], preferred_element_type=jnp.float32)
                att[h, b * 256:b * 256 + 256, :] = (
                    result[:, 0:HD] / result[:, HD:]
                ).astype(jnp.bfloat16)

        for h in heads:
            one(h)
        for h in heads:
            out_copy(h).start()

    def out_copy(h):
        return pltpu.make_async_copy(att.at[h], attended.at[:, pl.ds(h * HD, HD)], out_s.at[h])

    def page_own(step):
        if step == 0:
            return pltpu.make_async_copy(p1.at[x], p2.at[x], page_l.at[0])
        if step == 1:
            return pltpu.make_async_copy(p2.at[:, y], p3.at[pl.ds(y * 4, 4)], page_l.at[1])
        return pltpu.make_async_copy(p3.at[:, z], p4.at[pl.ds(z * 16, 16)], page_l.at[2])

    def page_start(step):
        axis = "xyz"[step]
        page_own(step).start()
        for d in (1, 3, 2):
            i = (coords[axis] + d) % 4
            if step == 0:
                src, dst = p1.at[i], p2.at[x]
            elif step == 1:
                src, dst = p2.at[:, i], p3.at[pl.ds(y * 4, 4)]
            else:
                src, dst = p3.at[:, i], p4.at[pl.ds(z * 16, 16)]
            remote(src, dst, page_s.at[step], page_r.at[step], axis, i)

    def page_wait(step, sem):
        wait((p2.at[0:3], p3.at[0:12], p4.at[0:48])[step], sem.at[step])

    def page_take(step):
        page_own(step).wait()
        page_wait(step, page_r)

    anchor_steps = (
        ("x", m0, r0), ("y", m1, r1), ("z", None, r2), ("y", None, r3), ("x", None, r4),
    )

    def anchor_start(step):
        axis, parts, to = anchor_steps[step]
        i = coords[axis]
        if step == 0:
            r0[x] = m0[x]
        elif step == 1:
            total = r0[0] + r0[1] + r0[2] + r0[3]
            m1[...] = total.reshape(4, 64, HD)
            r1[y] = m1[y]
        elif step == 2:
            r2[z] = r1[0] + r1[1] + r1[2] + r1[3]
        elif step == 3:
            r3[y] = r2[0] + r2[1] + r2[2] + r2[3]
        else:
            r4[x] = r3[...].reshape(256, HD)
        for d in (1, 3, 2):
            j = (i + d) % 4
            src = parts.at[j] if parts is not None else to.at[i]
            remote(src, to.at[i], anc_s.at[step], anc_r.at[step], axis, j)

    def anchor_wait(step, sem):
        wait(anchor_steps[step][2].at[0:3], sem.at[step])

    def anchor_take(step):
        anchor_wait(step, anc_r)

    def keys_values():
        project(all_hidden, 0, wkv, 16)
        key = rotated(acc[:, :HD]).astype(jnp.bfloat16)
        value = acc[:, HD:].astype(jnp.bfloat16)
        wide_key, wide_value = key.astype(jnp.float32), value.astype(jnp.float32)
        kt[:, TOK:] = wide_key.T.astype(jnp.bfloat16)
        vs[TOK:, 0:HD] = value
        m0[0:2] = (wide_key * root).astype(jnp.bfloat16).reshape(2, 256, HD)
        m0[2:4] = (wide_value * root).astype(jnp.bfloat16).reshape(2, 256, HD)
        pg[:, 0:HD] = key
        pg[:, HD:] = value

    def angles():
        row = lax.broadcasted_iota(jnp.int32, (TOK, HD), 0)
        angle = (my_block * TOK + row).astype(jnp.float32) * inverse[...]
        lane = lax.broadcasted_iota(jnp.int32, (TOK, HD), 1)
        cosine[...] = jnp.cos(angle)
        turned = jnp.sin(angle)
        sine[...] = jnp.where(lane < HD // 2, -turned, turned)

    def spread_lanes(count, width, value_of):
        lane = lax.broadcasted_iota(jnp.int32, (1, count * width), 1)

        def one(k, row):
            return jnp.where(lane // width == k, value_of(k), row)

        return lane, lax.fori_loop(0, count, one, jnp.zeros_like(lane))

    def one_hot(rows, target):
        row = lax.broadcasted_iota(jnp.int32, (rows, target.shape[1]), 0)
        return jnp.where(row == target, 1.0, 0.0).astype(jnp.bfloat16)

    def page_targets():
        def owner(j):
            return page_map[my_block * 64 + j]

        lane, owners = spread_lanes(64, PAGE, owner)

        def rank(j, total):
            later = (owners == owner(j)) & (lane // PAGE > j)
            return total + jnp.where(later, 1, 0)

        ranks = lax.fori_loop(0, 64, rank, jnp.zeros_like(owners))
        to_owner[...] = (owners * 2 + ranks) * PAGE + lane % PAGE
        lane, blocks = spread_lanes(
            64, 16, lambda a: block_order[(a % 4) * 16 + (a // 4) % 4 * 4 + a // 16]
        )
        to_block[...] = blocks * 16 + lane % 16

    def deal_pages():
        dealt = jnp.dot(
            one_hot(1024, to_owner[...]), pg[...], preferred_element_type=jnp.float32
        )
        p1[...] = dealt.astype(jnp.bfloat16).reshape(4, 4, 4, 16, 2 * HD)

    def place_pages():
        placed = jnp.dot(
            one_hot(1024, to_block[...]), p4[...].reshape(1024, 2 * HD),
            preferred_element_type=jnp.float32,
        )
        kvo[...] = placed.astype(jnp.bfloat16).reshape(64, 16, 2 * HD)

    kv_copy = pltpu.make_async_copy(kvo, kv_cache, out_s.at[8])

    def each(f, *groups):
        for g in groups:
            f(g)

    each(a_start, 0, 1)
    for g in range(2, 10):
        own_copy(g).start()
    lax.fori_loop(0, 64, hid_load, 0)
    for g in (0, 1):
        a_wait(g)
        b_start(g)
    each(a_start, *range(2, 10))
    wait(hid, hid_l.at[0])
    each(hid_start, 0, 1, 2, 3)
    each(b_pass, 0, 1)
    for g in (0, 1):
        b_wait(g)
        c_start(g)
    for g in (2, 3):
        a_wait(g)
        b_start(g)
    page_targets()
    angles()
    each(c_pass, 0, 1)
    for g in (4, 5):
        a_wait(g)
        b_start(g)
    each(b_pass, 2, 3)
    for g in (2, 3):
        b_wait(g)
        c_start(g)
    each(b_pass, 4, 5)
    hid_pass(0)
    each(c_wait, 0, 1)
    keys_values()
    anchor_start(0)
    each(c_pass, 2, 3)
    for g in (6, 7):
        a_wait(g)
        b_start(g)
    deal_pages()
    page_start(0)
    each(b_wait, 4, 5)
    hid_pass(1)
    each(c_start, 4, 5)
    each(b_pass, 6, 7)
    anchor_take(0)
    anchor_start(1)
    each(c_wait, 2, 3)
    hid_pass(2)
    parts_own(2)
    each(c_pass, 4, 5)
    for g in (8, 9):
        a_wait(g)
        b_start(g)
    page_take(0)
    page_start(1)
    anchor_take(1)
    anchor_start(2)
    each(b_wait, 6, 7)
    hid_pass(3)
    each(c_start, 6, 7)
    each(b_pass, 8, 9)
    anchor_take(2)
    anchor_start(3)
    page_take(1)
    page_start(2)
    each(c_wait, 4, 5)
    each(c_pass, 6, 7)
    wait(hid_p.at[0:2], core_r.at[0])
    parts_other(2)
    parts_other(4)
    for g in (8, 9):
        b_wait(g)
        c_start(g)
    anchor_take(3)
    anchor_start(4)
    parts_own(4)
    each(c_wait, 6, 7)
    parts_other(6)
    each(c_pass, 8, 9)
    parts_own(6)
    anchor_take(4)
    anchor_ready()
    queries(2)
    attend(0, 1)
    queries(4)
    attend(2, 3)
    each(c_wait, 8, 9)
    parts_other(8)
    parts_own(8)
    queries(6)
    attend(4, 5)
    page_take(2)
    place_pages()
    kv_copy.start()
    for h in (6, 7):
        query(h)
        attend(h)

    for g in range(10):
        a_done(g, send.at[g, 0])
        wait(layout(g, 1)[2](3), send.at[g, 1])
        wait(layout(g, 2)[2](3), send.at[g, 2])
    wait(hid_p.at[0:2], hid_s.at[0])
    wait(hid_p.at[0:2], core_s.at[0])
    for h in range(8):
        part_wait(h, par_s)
    for step in range(3):
        page_wait(step, page_s)
    for step in range(5):
        anchor_wait(step, anc_s)
    for h in range(8):
        out_copy(h).wait()
    kv_copy.wait()


def on_device(hidden, w_query, w_key, w_value, block_order, page_map):
    ctx_count = lax.axis_size("ctx")
    exponent = np.arange(HD, dtype=np.float64) % (HD // 2) * (2.0 / HD)
    inverse = jnp.asarray((rope_theta ** -exponent).astype(np.float32)[None, :])

    hbm = pl.BlockSpec(memory_space=pl.ANY)
    vmem = pl.BlockSpec(memory_space=pltpu.VMEM)
    smem = pl.BlockSpec(memory_space=pltpu.SMEM)
    bf16, f32, dma = jnp.bfloat16, jnp.float32, pltpu.SemaphoreType.DMA
    attended, kv = pl.pallas_call(
        kernel,
        out_shape=(
            jax.ShapeDtypeStruct((TOK, 8 * HD), bf16),
            jax.ShapeDtypeStruct((64, 16, 2 * HD), bf16),
        ),
        in_specs=[hbm] * 4 + [vmem] + [smem] * 2,
        out_specs=(hbm, hbm),
        scratch_shapes=[
            pltpu.VMEM((2, 4, 4, 4, HD, HD), bf16),
            pltpu.VMEM((8, 4, 4, 2, HD, HD), bf16),
            pltpu.VMEM((4, 4, 2, 2, TOK, HD), bf16),
            pltpu.VMEM((4, 4, 2, TOK, HD), bf16),
            pltpu.VMEM((TOK, 2 * HD), f32),
            pltpu.VMEM((8, TOK, HD), f32),
            pltpu.VMEM((8, TOK, HD), bf16),
            pltpu.VMEM((8, TOK, HD), bf16),
            pltpu.VMEM((TOK, HD), f32),
            pltpu.VMEM((TOK, HD), f32),
            pltpu.VMEM((HD, 2 * TOK), bf16),
            pltpu.VMEM((2 * TOK, 2 * HD), bf16),
            pltpu.VMEM((8, TOK, HD), bf16),
            pltpu.VMEM((8, TOK, HD), bf16),
            pltpu.VMEM((TOK, 2 * HD), bf16),
            pltpu.VMEM((4, 4, 4, 16, 2 * HD), bf16),
            pltpu.VMEM((4, 4, 4, 16, 2 * HD), bf16),
            pltpu.VMEM((16, 4, 16, 2 * HD), bf16),
            pltpu.VMEM((64, 16, 2 * HD), bf16),
            pltpu.VMEM((4, 256, HD), bf16),
            pltpu.VMEM((4, 256, HD), bf16),
            pltpu.VMEM((4, 64, HD), bf16),
            pltpu.VMEM((4, 64, HD), bf16),
            pltpu.VMEM((4, 64, HD), bf16),
            pltpu.VMEM((4, 64, HD), bf16),
            pltpu.VMEM((4, 256, HD), bf16),
            pltpu.VMEM((64, 16, 2 * HD), bf16),
            pltpu.VMEM((1, TOK), jnp.int32),
            pltpu.VMEM((1, 1024), jnp.int32),
            dma((10,)),
            dma((1,)),
            dma((10, 3)),
            dma((10,)),
            dma((10, 3)),
            dma((10, 3)),
            dma((1,)),
            dma((4,)),
            dma((1,)),
            dma((1,)),
            dma((8,)),
            dma((8,)),
            dma((3,)),
            dma((3,)),
            dma((3,)),
            dma((5,)),
            dma((5,)),
            dma((9,)),
        ],
        compiler_params=pltpu.CompilerParams(
            collective_id=0, has_side_effects=True, vmem_limit_bytes=56 * 1024 * 1024
        ),
        cost_estimate=pl.CostEstimate(
            flops=2 * TOK * 8192 * 1280, bytes_accessed=12 << 20, transcendentals=8 * TOK * 1024
        ),
    )(hidden, w_query, w_key, w_value, inverse, block_order, page_map[:, 0])
    return attended, kv.reshape(1, ctx_count, 2, PAGE, 2 * HD)


def solution(mesh):
    placed = (P("ctx", None), P("ctx", "tp"), P("ctx", "tp"), P("ctx", "tp"), P(), P())
    return jax.shard_map(
        on_device,
        mesh=mesh,
        in_specs=placed,
        out_specs=(P("ctx", "tp"), P("ctx", None, None, None, "tp")),
        check_vma=False,
    )
```
